32 devices in a mesh: dp: 2 (over x), ctx: 4 (over z), fsdp: 4 (over y, core).
Axes of the slice: x: 2, y: 2, z: 4, core: 2. Of those that a mesh axis runs over, the one named last changes fastest.
Arguments:
- tokens: bfloat16 [8, 1024, 2048], P(('dp', 'fsdp'), 'ctx'), may hold values from -6 to 6
- segment_ids: int32 [8, 1024], P(('dp', 'fsdp'), 'ctx'), may hold values from 0 to 1023, as said below
- cotangent: bfloat16 [8, 1024, 2048], P(('dp', 'fsdp'), 'ctx')
- query_master: float32 [2048, 2048], P(('dp', 'ctx', 'fsdp')), may hold values from -0.125 to 0.125
- query_first: float32 [2048, 2048], P(('dp', 'ctx', 'fsdp'))
- query_second: float32 [2048, 2048], P(('dp', 'ctx', 'fsdp'))
- key_master: float32 [2048, 512], P(('dp', 'ctx', 'fsdp')), may hold values from -0.125 to 0.125
- key_first: float32 [2048, 512], P(('dp', 'ctx', 'fsdp'))
- key_second: float32 [2048, 512], P(('dp', 'ctx', 'fsdp'))
- value_master: float32 [2048, 512], P(('dp', 'ctx', 'fsdp')), may hold values from -0.125 to 0.125
- value_first: float32 [2048, 512], P(('dp', 'ctx', 'fsdp'))
- value_second: float32 [2048, 512], P(('dp', 'ctx', 'fsdp'))
- output_master: float32 [2048, 2048], P(('dp', 'ctx', 'fsdp')), may hold values from -0.75 to 0.75
- output_first: float32 [2048, 2048], P(('dp', 'ctx', 'fsdp'))
- output_second: float32 [2048, 2048], P(('dp', 'ctx', 'fsdp'))
- gate_master: float32 [2048, 8192], P(('dp', 'ctx', 'fsdp')), may hold values from -0.125 to 0.125
- gate_first: float32 [2048, 8192], P(('dp', 'ctx', 'fsdp'))
- gate_second: float32 [2048, 8192], P(('dp', 'ctx', 'fsdp'))
- up_master: float32 [2048, 8192], P(('dp', 'ctx', 'fsdp')), may hold values from -0.125 to 0.125
- up_first: float32 [2048, 8192], P(('dp', 'ctx', 'fsdp'))
- up_second: float32 [2048, 8192], P(('dp', 'ctx', 'fsdp'))
- down_master: float32 [2048, 8192], P(('dp', 'ctx', 'fsdp')), may hold values from -0.0625 to 0.0625
- down_first: float32 [2048, 8192], P(('dp', 'ctx', 'fsdp'))
- down_second: float32 [2048, 8192], P(('dp', 'ctx', 'fsdp'))
- norm_gains: float32 [4224], replicated
- gains_first: float32 [4224], replicated
- gains_second: float32 [4224], replicated
Outputs:
- output: bfloat16 [8, 1024, 2048], P(('dp', 'fsdp'), 'ctx')
- input_grad: float32 [8, 1024, 2048], P(('dp', 'fsdp'), 'ctx')
- query_first_new: float32 [2048, 2048], P(('dp', 'ctx', 'fsdp'))
- query_second_new: float32 [2048, 2048], P(('dp', 'ctx', 'fsdp'))
- query_new: float32 [2048, 2048], P(('dp', 'ctx', 'fsdp'))
- key_first_new: float32 [2048, 512], P(('dp', 'ctx', 'fsdp'))
- key_second_new: float32 [2048, 512], P(('dp', 'ctx', 'fsdp'))
- key_new: float32 [2048, 512], P(('dp', 'ctx', 'fsdp'))
- value_first_new: float32 [2048, 512], P(('dp', 'ctx', 'fsdp'))
- value_second_new: float32 [2048, 512], P(('dp', 'ctx', 'fsdp'))
- value_new: float32 [2048, 512], P(('dp', 'ctx', 'fsdp'))
- output_first_new: float32 [2048, 2048], P(('dp', 'ctx', 'fsdp'))
- output_second_new: float32 [2048, 2048], P(('dp', 'ctx', 'fsdp'))
- output_new: float32 [2048, 2048], P(('dp', 'ctx', 'fsdp'))
- gate_first_new: float32 [2048, 8192], P(('dp', 'ctx', 'fsdp'))
- gate_second_new: float32 [2048, 8192], P(('dp', 'ctx', 'fsdp'))
- gate_new: float32 [2048, 8192], P(('dp', 'ctx', 'fsdp'))
- up_first_new: float32 [2048, 8192], P(('dp', 'ctx', 'fsdp'))
- up_second_new: float32 [2048, 8192], P(('dp', 'ctx', 'fsdp'))
- up_new: float32 [2048, 8192], P(('dp', 'ctx', 'fsdp'))
- down_first_new: float32 [2048, 8192], P(('dp', 'ctx', 'fsdp'))
- down_second_new: float32 [2048, 8192], P(('dp', 'ctx', 'fsdp'))
- down_new: float32 [2048, 8192], P(('dp', 'ctx', 'fsdp'))
- gains_first_new: float32 [4224], replicated
- gains_second_new: float32 [4224], replicated
- gains_new: float32 [4224], replicated
- grad_norm: float32 [], replicated
The draws below stay inside these ranges and needn't reach their ends.
Inputs may be any that keep to these rules, and one draw needn't show every extreme that they name: `segment_ids`: along each sequence the ids never fall, and each token's id is the index of the first token of its document; one document of every sequence begins within its first 256 tokens and ends within its last 256; the last token of every sequence begins a document.
All inputs are finite; a program needn't handle non-finite values.
Results may differ from the reference program's by a relative error of at most 0.018.
Values may be sent and summed in bfloat16 or wider, within the bound.
No kernel may reach another device: no remote copies, remote signals or barrier semaphores. Data moves between devices by JAX's collectives and lax.ppermute only.
A program may use at most 768 MiB of HBM per device.

```python
import jax
import jax.numpy as jnp
from jax import lax

D = 2048
H = 32
HD = 64
KVH = 8
FF = 8192
CTX_TOK = 256
STEP = 10
SEQS = 8
SEQ_LEN = 1024
N_DP = 2
N_CTX = 4
N_FSDP = 4
DEVICES = 32


clip_bound = 1.0


def axis_rise(width, ratio):
    device = jnp.arange(width, dtype=jnp.int32) // (width // DEVICES)
    inner = (device % N_FSDP).astype(jnp.float32) / max(N_FSDP - 1, 1)
    middle = (device // N_FSDP % N_CTX).astype(jnp.float32) / max(N_CTX - 1, 1)
    outer = (device // (N_FSDP * N_CTX)).astype(jnp.float32) / max(N_DP - 1, 1)
    return ratio ** (0.5 * (inner + middle + outer))


def grad_entry(factor):
    params = D * (2 * H * HD + 2 * KVH * HD + 3 * FF) + 2 * D + 2 * HD
    return factor * clip_bound / params ** 0.5


def first_moment(key, shape, factor):
    return 0.11 * grad_entry(factor) * jax.random.normal(key, shape, jnp.float32)


def second_moment(key, shape, factor):
    spread = jax.random.uniform(key, shape, jnp.float32)
    return 0.053 * grad_entry(factor) ** 2 * 4.0 ** spread


def draw_segment_ids(key, part):
    key = jax.random.fold_in(key, 11)
    keys = jax.random.split(key, 4)
    length = SEQ_LEN
    begin = jax.random.randint(keys[0], (SEQS, 1), 1, CTX_TOK)
    finish = jax.random.randint(keys[1], (SEQS, 1), length - CTX_TOK + 1, length - 1)
    period = jax.random.randint(keys[2], (SEQS, 1), 4, 40)
    marks = jax.random.randint(keys[3], (SEQS, length), 0, 1 << 20) % period == 0
    place = jnp.arange(length, dtype=jnp.int32)[None, :]
    inside = (place > begin) & (place < finish)
    starts = marks & ~inside | (place == 0) | (place == begin) | (place == finish) | (place == length - 1)
    return lax.cummax(jnp.where(starts, place, 0), axis=1).astype(jnp.int32)


def draw_cotangent(key, part):
    key = jax.random.fold_in(key, 7)
    base = jax.random.normal(key, (SEQS, SEQ_LEN, D), jnp.float32)
    rise = axis_rise(D, 3.0)
    return (0.5 * base * rise).astype(jnp.bfloat16)


def draw_norm_gains(key, part):
    key = jax.random.fold_in(key, 5)
    keys = jax.random.split(key, 4)
    rise = axis_rise(D, 3.0)
    lower, upper = (0.8, 1.25)
    first = 0.5 * rise * jax.random.uniform(keys[0], (D,), jnp.float32, lower, upper)
    second = 0.5 * rise * jax.random.uniform(keys[1], (D,), jnp.float32, lower, upper)
    query = jax.random.uniform(keys[2], (HD,), jnp.float32, 0.9, 1.5)
    keyed = jax.random.uniform(keys[3], (HD,), jnp.float32, 0.9, 1.5)
    return jnp.concatenate([first, second, query, keyed])


def draw_query_first(key, part):
    key = jax.random.fold_in(key, 21)
    return first_moment(key, (D, H * HD), 1.0)


def draw_query_second(key, part):
    key = jax.random.fold_in(key, 22)
    return second_moment(key, (D, H * HD), 1.0)


def draw_key_first(key, part):
    key = jax.random.fold_in(key, 23)
    return first_moment(key, (D, KVH * HD), 1.0)


def draw_key_second(key, part):
    key = jax.random.fold_in(key, 24)
    return second_moment(key, (D, KVH * HD), 1.0)


def draw_value_first(key, part):
    key = jax.random.fold_in(key, 25)
    return first_moment(key, (D, KVH * HD), 1.0)


def draw_value_second(key, part):
    key = jax.random.fold_in(key, 26)
    return second_moment(key, (D, KVH * HD), 1.0)


def draw_output_first(key, part):
    key = jax.random.fold_in(key, 27)
    return first_moment(key, (D, H * HD), 1.0)


def draw_output_second(key, part):
    key = jax.random.fold_in(key, 28)
    return second_moment(key, (D, H * HD), 1.0)


def draw_gate_first(key, part):
    key = jax.random.fold_in(key, 29)
    return first_moment(key, (D, FF), 1.0)


def draw_gate_second(key, part):
    key = jax.random.fold_in(key, 30)
    return second_moment(key, (D, FF), 1.0)


def draw_up_first(key, part):
    key = jax.random.fold_in(key, 31)
    return first_moment(key, (D, FF), 1.0)


def draw_up_second(key, part):
    key = jax.random.fold_in(key, 32)
    return second_moment(key, (D, FF), 1.0)


def draw_down_first(key, part):
    key = jax.random.fold_in(key, 33)
    return first_moment(key, (D, FF), 1.0)


def draw_down_second(key, part):
    key = jax.random.fold_in(key, 34)
    return second_moment(key, (D, FF), 1.0)


def draw_gains_first(key, part):
    key = jax.random.fold_in(key, 35)
    return first_moment(key, (2 * D + 2 * HD,), 3.0)


def draw_gains_second(key, part):
    key = jax.random.fold_in(key, 36)
    return second_moment(key, (2 * D + 2 * HD,), 3.0)


def levels(key, extent, cuts, smallest, largest):
    level, own = 1.0, jax.random.fold_in(key, 6)
    for axis_at, blocks in cuts:
        draws = jnp.exp(jax.random.uniform(jax.random.fold_in(own, axis_at), (blocks,), jnp.float32, smallest / len(cuts), largest / len(cuts)))
        level = level * jnp.repeat(draws, extent[axis_at] // blocks).reshape([-1 if axis == axis_at else 1 for axis in range(len(extent))])
    return level


def centred(rng, dims, deviation, most, cuts=(), kind=jnp.bfloat16):
    entries = deviation * jax.random.normal(rng, dims, jnp.float32)
    if cuts:
        entries = entries * levels(rng, dims, cuts, -0.22, 0.18)
    return jnp.clip(entries, -most, most).astype(kind)


def setup_inputs(seed: int = 0) -> dict:
    streams_of = jax.random.split(jax.random.key(seed), 28)
    return {
        "tokens": centred(streams_of[0], (SEQS, SEQ_LEN, D), 1.0, 6.0, ((0, 8), (1, 4))),
        "segment_ids": draw_segment_ids(jax.random.fold_in(streams_of[27], 71), 0),
        "cotangent": draw_cotangent(jax.random.fold_in(streams_of[27], 71), 0),
        "query_master": centred(streams_of[3], (D, H * HD), D ** -0.5, 0.125, ((0, 32),), jnp.float32),
        "query_first": draw_query_first(jax.random.fold_in(streams_of[27], 71), 0),
        "query_second": draw_query_second(jax.random.fold_in(streams_of[27], 71), 0),
        "key_master": centred(streams_of[6], (D, KVH * HD), D ** -0.5, 0.125, ((0, 32),), jnp.float32),
        "key_first": draw_key_first(jax.random.fold_in(streams_of[27], 71), 0),
        "key_second": draw_key_second(jax.random.fold_in(streams_of[27], 71), 0),
        "value_master": centred(streams_of[9], (D, KVH * HD), D ** -0.5, 0.125, ((0, 32),), jnp.float32),
        "value_first": draw_value_first(jax.random.fold_in(streams_of[27], 71), 0),
        "value_second": draw_value_second(jax.random.fold_in(streams_of[27], 71), 0),
        "output_master": centred(streams_of[12], (D, H * HD), (H * HD // 32) ** -0.5, 0.75, ((0, 32),), jnp.float32),
        "output_first": draw_output_first(jax.random.fold_in(streams_of[27], 71), 0),
        "output_second": draw_output_second(jax.random.fold_in(streams_of[27], 71), 0),
        "gate_master": centred(streams_of[15], (D, FF), D ** -0.5, 0.125, ((0, 32),), jnp.float32),
        "gate_first": draw_gate_first(jax.random.fold_in(streams_of[27], 71), 0),
        "gate_second": draw_gate_second(jax.random.fold_in(streams_of[27], 71), 0),
        "up_master": centred(streams_of[18], (D, FF), D ** -0.5, 0.125, ((0, 32),), jnp.float32),
        "up_first": draw_up_first(jax.random.fold_in(streams_of[27], 71), 0),
        "up_second": draw_up_second(jax.random.fold_in(streams_of[27], 71), 0),
        "down_master": centred(streams_of[21], (D, FF), FF ** -0.5, 0.0625, ((0, 32),), jnp.float32),
        "down_first": draw_down_first(jax.random.fold_in(streams_of[27], 71), 0),
        "down_second": draw_down_second(jax.random.fold_in(streams_of[27], 71), 0),
        "norm_gains": draw_norm_gains(jax.random.fold_in(streams_of[27], 71), 0),
        "gains_first": draw_gains_first(jax.random.fold_in(streams_of[27], 71), 0),
        "gains_second": draw_gains_second(jax.random.fold_in(streams_of[27], 71), 0),
    }


eps_norm = 1e-05
rope_base = 1000000.0
clip_bound = 1.0
beta_one = 0.9
beta_two = 0.95
adam_eps = 1e-08
weight_decay = 0.1
weight_rate = 0.04
gain_rate = 0.4
masked = -1e+30

@jax.custom_vjp
def low(v):
    return lax.optimization_barrier(v.astype(jnp.bfloat16)).astype(jnp.float32)

@jax.custom_vjp
def low_back(v):
    return v

def low_keep(v):
    return (low(v), None)

def low_pass(kept, grad):
    return (grad,)

def back_keep(v):
    return (v, None)

def back_low(kept, grad):
    return (low(grad),)
low.defvjp(low_keep, low_pass)
low_back.defvjp(back_keep, back_low)

def matmul(left, right):
    return jnp.dot(left, right, precision=lax.Precision.HIGHEST, preferred_element_type=jnp.float32)

def rms_scale(values, gain):
    return values * lax.rsqrt(lax.optimization_barrier(jnp.mean(values * values, axis=-1, keepdims=True)) + eps_norm) * gain

def rope_tables(positions):
    half = HD // 2
    freq = rope_base ** (-(jnp.arange(half, dtype=jnp.float32) * 2.0 / HD))
    angle = positions.astype(jnp.float32)[:, None] * freq[None, :]
    return (jnp.cos(angle)[:, None, :], jnp.sin(angle)[:, None, :])

def rotate(values, cosine, sine):
    half = values.shape[-1] // 2
    first = values[..., :half]
    second = values[..., half:]
    return jnp.concatenate([first * cosine - second * sine, second * cosine + first * sine], axis=-1)

def attend(query, keys, values, doc_start):
    length = query.shape[0]
    place = jnp.arange(length, dtype=jnp.int32)
    allowed = (doc_start[:, None] == doc_start[None, :]) & (place[:, None] >= place[None, :])
    query_groups = query.reshape(length, KVH, H // KVH, HD).transpose(1, 0, 2, 3)
    key_groups = keys.reshape(length, KVH, HD).transpose(1, 0, 2)
    value_groups = values.reshape(length, KVH, HD).transpose(1, 0, 2)

    def one_head(items):
        query_head, key_head, value_head = items
        scores = jnp.einsum('lgd,md->glm', query_head, key_head, precision=lax.Precision.HIGHEST) * HD ** (-0.5)
        scores = low_back(scores)
        scores = jnp.where(allowed[None], scores, masked)
        top = lax.optimization_barrier(jnp.max(scores, axis=-1, keepdims=True))
        expd = jnp.exp(scores - top)
        probs = low(expd / lax.optimization_barrier(jnp.sum(expd, axis=-1, keepdims=True)))
        return jnp.einsum('glm,md->lgd', probs, value_head, precision=lax.Precision.HIGHEST)
    result = lax.map(jax.checkpoint(one_head), (query_groups, key_groups, value_groups))
    return result.transpose(1, 0, 2, 3).reshape(length, H * HD)

def block(inputs, doc_start, query_master, key_master, value_master, output_master, gate_master, up_master, down_master, norm_gains):
    length = inputs.shape[0]
    gain_one = norm_gains[:D]
    gain_two = norm_gains[D:2 * D]
    gain_query = norm_gains[2 * D:2 * D + HD]
    gain_key = norm_gains[2 * D + HD:]
    positions = jnp.arange(length, dtype=jnp.int32) - doc_start
    cosine, sine = rope_tables(positions)
    normed = low(rms_scale(inputs, gain_one))
    query_raw = low_back(matmul(normed, low(query_master)))
    key_raw = low_back(matmul(normed, low(key_master)))
    values = low(low_back(matmul(normed, low(value_master))))
    query = rotate(rms_scale(query_raw.reshape(length, H, HD), gain_query), cosine, sine)
    keys = rotate(rms_scale(key_raw.reshape(length, KVH, HD), gain_key), cosine, sine)
    query = low(query.reshape(length, H * HD))
    keys = low(keys.reshape(length, KVH * HD))
    attended = low(low_back(attend(query, keys, values, doc_start)))
    middle = inputs + low_back(matmul(attended, low(output_master).T))
    normed_two = low(rms_scale(middle, gain_two))
    gate = low_back(matmul(normed_two, low(gate_master)))
    upward = low_back(matmul(normed_two, low(up_master)))
    hidden = low(jax.nn.silu(gate) * upward)
    branch = low_back(matmul(hidden, low(down_master).T))
    return middle + branch

def adam_update(weight, grad, first, second, rate, decay):
    first_new = beta_one * first + (1.0 - beta_one) * grad
    second_new = beta_two * second + (1.0 - beta_two) * grad * grad
    ratio = first_new / (1.0 - beta_one ** STEP) / (jnp.sqrt(second_new / (1.0 - beta_two ** STEP)) + adam_eps)
    return (first_new, second_new, weight - rate * (ratio + decay * weight))

def reference(tokens, segment_ids, cotangent, query_master, query_first, query_second, key_master, key_first, key_second, value_master, value_first, value_second, output_master, output_first, output_second, gate_master, gate_first, gate_second, up_master, up_first, up_second, down_master, down_first, down_second, norm_gains, gains_first, gains_second):
    masters = (query_master, key_master, value_master, output_master, gate_master, up_master, down_master)
    firsts = (query_first, key_first, value_first, output_first, gate_first, up_first, down_first)
    seconds = (query_second, key_second, value_second, output_second, gate_second, up_second, down_second)

    def one_sequence(totals, items):
        seq_tokens, seq_starts, seq_back = items

        def forward(inputs, *params):
            return block(inputs, seq_starts, *params)
        result, pullback = jax.vjp(forward, seq_tokens.astype(jnp.float32), *masters, norm_gains)
        grads = pullback(seq_back.astype(jnp.float32))
        totals = tuple((total + grad for total, grad in zip(totals, grads[1:])))
        return (totals, (result.astype(jnp.bfloat16), grads[0]))
    initial = tuple((jnp.zeros(param.shape, jnp.float32) for param in masters + (norm_gains,)))
    totals, (output, input_grad) = lax.scan(one_sequence, initial, (tokens, segment_ids, cotangent))
    squares = jnp.float32(0.0)
    for grad in totals:
        squares = squares + jnp.sum(grad * grad)
    grad_norm = jnp.sqrt(squares)
    factor = jnp.minimum(1.0, clip_bound / (grad_norm + 1e-06))
    updated = []
    for master, first, second, grad in zip(masters, firsts, seconds, totals[:7]):
        updated.extend(adam_update(master, factor * grad, first, second, weight_rate, weight_decay))
    gains_done = adam_update(norm_gains, factor * totals[7], gains_first, gains_second, gain_rate, 0.0)
    return (output, input_grad, updated[0], updated[1], updated[2], updated[3], updated[4], updated[5], updated[6], updated[7], updated[8], updated[9], updated[10], updated[11], updated[12], updated[13], updated[14], updated[15], updated[16], updated[17], updated[18], updated[19], updated[20], gains_done[0], gains_done[1], gains_done[2], grad_norm)
```

```python
from functools import partial

import jax
import jax.numpy as jnp
from jax import lax
from jax.experimental import pallas as pl
from jax.experimental.pallas import tpu as pltpu
from jax.sharding import PartitionSpec as P

D = 2048
H = 32
HD = 64
KVH = 8
FF = 8192
STEP = 10


eps_norm = 1e-05
rope_base = 1000000.0
clip_bound = 1.0
beta_one = 0.9
beta_two = 0.95
adam_eps = 1e-08
weight_decay = 0.1
weight_rate = 0.04
gain_rate = 0.4
masked = -1e30

BF = jnp.bfloat16
F32 = jnp.float32
GROUP = KVH
QW = H * HD // GROUP
KW = HD
FW = FF // GROUP


class Plan:
    def __init__(self, mesh):
        shape = dict(mesh.shape)
        self.shape = shape
        if shape["dp"] * shape["fsdp"] == GROUP:
            self.tp = ("dp", "fsdp")
        elif shape["dp"] == GROUP:
            self.tp = ("dp",)
        elif shape["fsdp"] == GROUP:
            self.tp = ("fsdp",)
        else:
            raise ValueError("unsupported mesh")
        self.rest = tuple(a for a in ("ctx", "dp", "fsdp") if a not in self.tp)
        self.all = ("dp", "ctx", "fsdp")
        self.two_by_four = self.tp == ("dp", "fsdp") and shape["dp"] == 2

    def me(self):
        return lax.axis_index(self.tp)

    def swap(self, value, bits):
        return lax.ppermute(value, self.tp, [(i, i ^ bits) for i in range(GROUP)])

    def to_inner(self, value):
        lead = value.shape[:-1]
        sizes = [self.shape[a] for a in self.all]
        n = len(lead)
        shaped = value.reshape(*lead, *sizes, -1)
        order = [n + self.all.index(a) for a in self.rest + self.tp]
        return shaped.transpose(*range(n), *order, n + 3).reshape(value.shape)

    def to_outer(self, value):
        lead = value.shape[:-1]
        names = self.rest + self.tp
        sizes = [self.shape[a] for a in names]
        n = len(lead)
        shaped = value.reshape(*lead, *sizes, -1)
        order = [n + names.index(a) for a in self.all]
        return shaped.transpose(*range(n), *order, n + 3).reshape(value.shape)

    def gather(self, own):
        if not self.two_by_four:
            return [own] + [self.swap(own, r) for r in range(1, GROUP)]
        half = own.shape[0] // 2
        x1 = self.swap(own, 4)
        y1 = self.swap(own, 2)
        c1 = self.swap(own, 1)
        top = self.swap(y1[:half], 4)
        low = self.swap(x1[half:], 2)
        diag = jnp.concatenate([top, low], axis=0)
        return [own, c1, y1, self.swap(y1, 1), x1, self.swap(x1, 1), diag, self.swap(diag, 1)]

    def gather_far(self, own):
        if not self.two_by_four:
            return self.gather(own)
        return [own, self.swap(own, 2), self.swap(own, 4), self.swap(own, 6)]

    def gather_near(self, far):
        if not self.two_by_four:
            return far
        return [part for one in far for part in (one, self.swap(one, 1))]

    def scatter(self, blocks):
        if not self.two_by_four:
            total = blocks[0].astype(F32)
            for r in range(1, GROUP):
                total = total + self.swap(blocks[r], r).astype(F32)
            return total
        half = blocks[0].shape[0] // 2
        part = {
            r: blocks[r].astype(F32) + self.swap(blocks[r ^ 1], 1).astype(F32) for r in (6, 4, 2, 0)
        }
        diag = part[6].astype(BF)
        top = self.swap(diag[:half], 4).astype(F32)
        low = self.swap(diag[half:], 2).astype(F32)
        by_y = jnp.concatenate([part[2][:half] + top, part[2][half:]], axis=0).astype(BF)
        by_x = jnp.concatenate([part[4][:half], part[4][half:] + low], axis=0).astype(BF)
        return part[0] + self.swap(by_y, 2).astype(F32) + self.swap(by_x, 4).astype(F32)

    def exchange(self, pick):
        me = self.me()
        return [pick(me)] + [self.swap(pick(me ^ r), r) for r in range(1, GROUP)]

    def weight_block(self, rows):
        width = rows.shape[1] // GROUP

        def pick(p):
            return lax.dynamic_slice_in_dim(rows, p * width, width, 1)

        return place(self.me().reshape(1), self.exchange(pick)).reshape(-1, width)

    def weight_rows(self, block):
        return lax.all_gather(block, self.rest, axis=0, tiled=True)

    def grad_sum(self, grad):
        mine = lax.psum_scatter(grad, self.rest, scatter_dimension=0, tiled=True)
        return mine.reshape(GROUP, -1, grad.shape[1])

    def grad_rows(self, mine):
        got = self.exchange(lambda p: lax.dynamic_index_in_dim(mine, p, 0, keepdims=False))
        return place(self.me().reshape(1), got, columns=True)

    def total(self, value):
        for axes in (self.tp,) + tuple((a,) for a in self.rest):
            size = 1
            for a in axes:
                size *= self.shape[a]
            step = 1
            while step < size:
                value = value + lax.ppermute(value, axes, [(i, i ^ step) for i in range(size)])
                step *= 2
        return value


def rms_scale(values, gain):
    return values * lax.rsqrt(jnp.mean(values * values, axis=-1, keepdims=True) + eps_norm) * gain


def rope_tables(positions):
    half = HD // 2
    freq = rope_base ** (-(jnp.arange(half, dtype=jnp.float32) * 2.0 / HD))
    angle = positions.astype(jnp.float32)[:, None] * freq[None, :]
    cosine, sine = jnp.cos(angle), jnp.sin(angle)
    return (
        jnp.concatenate([cosine] * 4, axis=1),
        jnp.concatenate([-sine, sine, -sine, sine], axis=1),
    )


def across(left, right):
    return lax.dot_general(
        left, right, (((0,), (0,)), ((), ())), preferred_element_type=jnp.float32
    )


def against(left, right):
    return lax.dot_general(
        left, right, (((1,), (1,)), ((), ())), preferred_element_type=jnp.float32
    )


def plain(left, right):
    return jnp.dot(left, right, preferred_element_type=jnp.float32)


def adam_update(weight, grad, first, second, rate, decay):
    first_new = beta_one * first + (1.0 - beta_one) * grad
    second_new = beta_two * second + (1.0 - beta_two) * grad * grad
    ratio = (
        first_new
        / (1.0 - beta_one**STEP)
        / (jnp.sqrt(second_new / (1.0 - beta_two**STEP)) + adam_eps)
    )
    return (first_new, second_new, weight - rate * (ratio + decay * weight))


LANES = 2 * HD


def cost(time):
    return pl.CostEstimate(flops=int(time * 5e8), bytes_accessed=1, transcendentals=0)


def swap_halves(values):
    width = values.shape[-1]
    lane = lax.broadcasted_iota(jnp.int32, values.shape, 1)
    ahead = pltpu.roll(values, width - HD // 2, 1)
    behind = pltpu.roll(values, HD // 2, 1)
    return jnp.where(lane % HD < HD // 2, ahead, behind)


def by_head(values):
    rows, width = values.shape
    return jnp.concatenate(
        [
            jnp.broadcast_to(
                jnp.mean(values[:, i : i + HD], axis=-1, keepdims=True), (rows, HD)
            )
            for i in range(0, width, HD)
        ],
        axis=1,
    )


def prepare_kernel(raw_ref, cos_ref, sin_ref, gain_ref, query_ref, kv_ref):
    raw = raw_ref[...]
    heads = raw.shape[1] // HD
    cosine = jnp.concatenate([cos_ref[...]] * (heads // 2), axis=1)
    sine = jnp.concatenate([sin_ref[...]] * (heads // 2), axis=1)
    normed = raw * lax.rsqrt(by_head(raw * raw) + eps_norm) * gain_ref[...]
    turned = normed * cosine + swap_halves(normed) * sine
    query_ref[...] = turned[:, :QW].astype(BF)
    tail = turned[:, QW:]
    lane = lax.broadcasted_iota(jnp.int32, tail.shape, 1)
    kv_ref[...] = jnp.where(lane < KW, tail, raw[:, QW:]).astype(BF)


def prepare(raw, cosine, sine, gains, tile):
    total, width = raw.shape
    return pl.pallas_call(
        prepare_kernel,
        grid=(total // tile,),
        in_specs=[
            pl.BlockSpec((tile, width), lambda i: (i, 0)),
            pl.BlockSpec((tile, LANES), lambda i: (i, 0)),
            pl.BlockSpec((tile, LANES), lambda i: (i, 0)),
            pl.BlockSpec((1, width), lambda i: (0, 0)),
        ],
        out_specs=[
            pl.BlockSpec((tile, QW), lambda i: (i, 0)),
            pl.BlockSpec((tile, LANES), lambda i: (i, 0)),
        ],
        out_shape=[
            jax.ShapeDtypeStruct((total, QW), BF),
            jax.ShapeDtypeStruct((total, LANES), BF),
        ],
        compiler_params=pltpu.CompilerParams(vmem_limit_bytes=24 << 20),
        cost_estimate=cost(6),
    )(raw, cosine, sine, gains)


def unprepare_kernel(n_ctx, raw_ref, cos_ref, sin_ref, gain_ref, dq_ref, *refs):
    parts, (out_ref, dgain_ref) = refs[:n_ctx], refs[n_ctx:]
    raw = raw_ref[...]
    heads = raw.shape[1] // HD
    cosine = jnp.concatenate([cos_ref[...]] * (heads // 2), axis=1)
    sine = jnp.concatenate([sin_ref[...]] * (heads // 2), axis=1)
    gain = gain_ref[...]
    dkv = parts[0][...]
    for part in parts[1:]:
        dkv = dkv + part[...].astype(F32)
    upper = jnp.concatenate([dq_ref[...], dkv], axis=1)
    dnormed = upper * cosine + swap_halves(upper * sine)
    scale = lax.rsqrt(by_head(raw * raw) + eps_norm)
    dgain = dnormed * raw * scale
    inner = dnormed * gain
    draw = scale * inner - raw * (scale * scale * scale) * by_head(inner * raw)
    lane = lax.broadcasted_iota(jnp.int32, upper.shape, 1)
    out_ref[...] = jnp.where(lane < QW + KW, draw, upper).astype(BF)
    total = jnp.sum(dgain, axis=0, keepdims=True)

    @pl.when(pl.program_id(0) == 0)
    def _():
        dgain_ref[...] = total

    @pl.when(pl.program_id(0) > 0)
    def _():
        dgain_ref[...] += total


def unprepare(raw, cosine, sine, gains, dquery, dkv, tile):
    total, width = raw.shape
    kv_spec = pl.BlockSpec((tile, LANES), lambda i: (i, 0))
    return pl.pallas_call(
        partial(unprepare_kernel, len(dkv)),
        grid=(total // tile,),
        in_specs=[
            pl.BlockSpec((tile, width), lambda i: (i, 0)),
            kv_spec,
            kv_spec,
            pl.BlockSpec((1, width), lambda i: (0, 0)),
            pl.BlockSpec((tile, QW), lambda i: (i, 0)),
        ]
        + [kv_spec] * len(dkv),
        out_specs=[
            pl.BlockSpec((tile, width), lambda i: (i, 0)),
            pl.BlockSpec((1, width), lambda i: (0, 0)),
        ],
        out_shape=[
            jax.ShapeDtypeStruct((total, width), BF),
            jax.ShapeDtypeStruct((1, width), F32),
        ],
        compiler_params=pltpu.CompilerParams(vmem_limit_bytes=24 << 20),
        cost_estimate=cost(11),
    )(raw, cosine, sine, gains, dquery, *dkv)


def allowed_bias(base, start, n_ctx, length):
    shape = (n_ctx * length, length)
    key = lax.broadcasted_iota(jnp.int32, shape, 0)
    key_place = base + key % length - (key // length) * length
    place = base + lax.broadcasted_iota(jnp.int32, shape, 1)
    return jnp.where((key_place >= start) & (key_place <= place), 0.0, masked)


def by_rows(left, right):
    return lax.dot_general(
        left, right, (((1,), (1,)), ((), ())), preferred_element_type=jnp.float32
    )


def flash_forward_kernel(n_ctx, base_ref, start_ref, query_ref, *refs):
    kv_refs, (out_ref, log_ref) = refs[:n_ctx], refs[n_ctx:]
    length = query_ref.shape[0]
    kv = jnp.concatenate([ref[...] for ref in kv_refs], axis=0)
    keys, values = kv[:, :HD], kv[:, HD:]
    values_t = values.T
    bias = allowed_bias(base_ref[0], start_ref[0], n_ctx, length)
    outs, logs = [], []
    for head in range(QW // HD):
        query = query_ref[:, head * HD : (head + 1) * HD] * BF(HD**-0.5)
        scores = by_rows(keys, query) + bias
        top = jnp.max(scores, axis=0, keepdims=True)
        weights = jnp.exp(scores - top)
        total = jnp.sum(weights, axis=0, keepdims=True)
        probs = (weights * (1.0 / total)).astype(BF)
        outs.append(jnp.dot(values_t, probs, preferred_element_type=F32))
        logs.append(top + jnp.log(total))
    out_ref[...] = jnp.concatenate(outs, axis=0).T.astype(BF)
    log_ref[0] = jnp.concatenate(logs, axis=0)


def flash_forward(base, starts, query, kv, length):
    total = query.shape[0]
    blocks = total // length
    heads = QW // HD
    n_ctx = len(kv)
    return pl.pallas_call(
        partial(flash_forward_kernel, n_ctx),
        grid=(blocks,),
        in_specs=[
            pl.BlockSpec(memory_space=pltpu.SMEM),
            pl.BlockSpec((1, 1, length), lambda i: (i, 0, 0)),
            pl.BlockSpec((length, QW), lambda i: (i, 0)),
        ]
        + [pl.BlockSpec((length, LANES), lambda i: (i, 0))] * n_ctx,
        out_specs=[
            pl.BlockSpec((length, QW), lambda i: (i, 0)),
            pl.BlockSpec((1, heads, length), lambda i: (i, 0, 0)),
        ],
        out_shape=[
            jax.ShapeDtypeStruct((total, QW), BF),
            jax.ShapeDtypeStruct((blocks, heads, length), F32),
        ],
        compiler_params=pltpu.CompilerParams(vmem_limit_bytes=40 << 20),
        cost_estimate=cost(28),
    )(base, starts, query, *kv)


def flash_backward_kernel(n_ctx, base_ref, start_ref, log_ref, query_ref, upper_ref, *refs):
    kv_refs, dq_ref, dkv_refs = refs[:n_ctx], refs[n_ctx], refs[n_ctx + 1 :]
    length = query_ref.shape[0]
    kv = jnp.concatenate([ref[...] for ref in kv_refs], axis=0)
    keys, values = kv[:, :HD], kv[:, HD:]
    keys_t = keys.T
    bias = allowed_bias(base_ref[0], start_ref[0], n_ctx, length)
    dqs = []
    dkeys = dvalues = None
    for head in range(QW // HD):
        cols = slice(head * HD, (head + 1) * HD)
        query = query_ref[:, cols] * BF(HD**-0.5)
        upper = upper_ref[:, cols]
        scores = by_rows(keys, query) + bias
        probs = jnp.exp(scores - log_ref[0, head : head + 1, :])
        dprobs = by_rows(values, upper)
        delta = jnp.sum(probs * dprobs, axis=0, keepdims=True)
        dscores = (probs * (dprobs - delta)).astype(BF)
        dqs.append(jnp.dot(keys_t, dscores, preferred_element_type=F32) * HD**-0.5)
        dkey = jnp.dot(dscores, query, preferred_element_type=F32)
        dvalue = jnp.dot(probs.astype(BF), upper, preferred_element_type=F32)
        dkeys = dkey if dkeys is None else dkeys + dkey
        dvalues = dvalue if dvalues is None else dvalues + dvalue
    dq_ref[...] = jnp.concatenate(dqs, axis=0).T
    dkv = jnp.concatenate([dkeys, dvalues], axis=1)
    for s in range(n_ctx):
        dkv_refs[s][...] = dkv[s * length : (s + 1) * length].astype(dkv_refs[s].dtype)


def flash_backward(base, starts, logs, query, upper, kv, length):
    total = query.shape[0]
    blocks = total // length
    heads = QW // HD
    n_ctx = len(kv)
    kv_spec = pl.BlockSpec((length, LANES), lambda i: (i, 0))
    q_spec = pl.BlockSpec((length, QW), lambda i: (i, 0))
    return pl.pallas_call(
        partial(flash_backward_kernel, n_ctx),
        grid=(blocks,),
        in_specs=[
            pl.BlockSpec(memory_space=pltpu.SMEM),
            pl.BlockSpec((1, 1, length), lambda i: (i, 0, 0)),
            pl.BlockSpec((1, heads, length), lambda i: (i, 0, 0)),
            q_spec,
            q_spec,
        ]
        + [kv_spec] * n_ctx,
        out_specs=[q_spec] + [kv_spec] * n_ctx,
        out_shape=[jax.ShapeDtypeStruct((total, QW), F32)]
        + [jax.ShapeDtypeStruct((total, LANES), BF if s else F32) for s in range(n_ctx)],
        compiler_params=pltpu.CompilerParams(vmem_limit_bytes=48 << 20),
        cost_estimate=cost(35),
    )(base, starts, logs, query, upper, *kv)


def place_rows_kernel(me_ref, *refs):
    blocks, out_ref = refs[:GROUP], refs[GROUP]
    for r, block in enumerate(blocks):
        out_ref[me_ref[0] ^ r] = block[...]


def place_columns_kernel(me_ref, *refs):
    blocks, out_ref = refs[:GROUP], refs[GROUP]
    width = blocks[0].shape[1]
    for r, block in enumerate(blocks):
        start = pl.multiple_of((me_ref[0] ^ r) * width, width)
        out_ref[:, pl.ds(start, width)] = block[...]


def place(me, blocks, columns=False):
    rows, width = blocks[0].shape
    shape = (rows, GROUP * width) if columns else (GROUP, rows, width)
    return pl.pallas_call(
        place_columns_kernel if columns else place_rows_kernel,
        in_specs=[pl.BlockSpec(memory_space=pltpu.SMEM)]
        + [pl.BlockSpec(memory_space=pltpu.VMEM)] * GROUP,
        out_specs=pl.BlockSpec(memory_space=pltpu.VMEM),
        out_shape=jax.ShapeDtypeStruct(shape, blocks[0].dtype),
        cost_estimate=cost(2),
    )(me, *blocks)


def columns_kernel(epilogue, n_b, n_w, n_x, *refs):
    blocks, refs = refs[:n_b], refs[n_b:]
    weights, refs = refs[:n_w], refs[n_w:]
    extras, refs = refs[:n_x], refs[n_x:]
    outs, (held, sems) = refs[:-2], refs[-2:]
    length = blocks[0].shape[0]
    chunk = held.shape[0] // 4

    @pl.when(pl.program_id(0) == 0)
    def _():
        copies = [
            pltpu.make_async_copy(block, held.at[pl.ds(r * length, length)], sems.at[r])
            for r, block in enumerate(blocks)
        ]
        for copy in copies:
            copy.start()
        for copy in copies:
            copy.wait()

    @pl.loop(0, 4)
    def _(r):
        rows = pl.ds(pl.multiple_of(r * chunk, chunk), chunk)
        left = held[rows, :]
        sums = [jnp.dot(left, w[...], preferred_element_type=F32) for w in weights]
        for out, value in zip(outs, epilogue(sums, [x[rows, :] for x in extras])):
            out[rows, :] = value.astype(out.dtype)


def columns(blocks, weights, extras, outs, epilogue, tile):
    n_b = len(blocks)
    length, depth = blocks[0].shape
    total = n_b * length
    wide = weights[0].shape[1]
    by_tile = pl.BlockSpec((total, tile), lambda j: (0, j))
    return pl.pallas_call(
        partial(columns_kernel, epilogue, n_b, len(weights), len(extras)),
        grid=(wide // tile,),
        in_specs=[pl.BlockSpec(memory_space=pl.ANY)] * n_b
        + [pl.BlockSpec((depth, tile), lambda j: (0, j))] * len(weights)
        + [by_tile] * len(extras),
        out_specs=[by_tile] * len(outs) + [pl.BlockSpec((total, depth), lambda j: (0, 0))],
        out_shape=[jax.ShapeDtypeStruct((total, wide), kind) for kind in outs]
        + [jax.ShapeDtypeStruct((total, depth), BF)],
        scratch_shapes=[pltpu.SemaphoreType.DMA((n_b,))],
        compiler_params=pltpu.CompilerParams(vmem_limit_bytes=52 << 20),
        cost_estimate=cost(2 * total * depth * wide * len(weights) / 6e8 + 3),
    )(*blocks, *weights, *extras)


def back_kernel(n, picks, *refs):
    lefts, weights, outs = refs[:n], refs[n : 2 * n], refs[2 * n :]
    length = outs[0].shape[0]
    for r, out in zip(picks, outs):
        rows = slice(r * length, (r + 1) * length)
        total = by_rows(lefts[0][rows, :], weights[0][...])
        for left, weight in zip(lefts[1:], weights[1:]):
            total = total + by_rows(left[rows, :], weight[...])
        out[...] = total.astype(BF)


def back(lefts, weights, tile, picks=tuple(range(GROUP))):
    total, wide = lefts[0].shape
    depth = weights[0].shape[0]
    length = total // GROUP
    n = len(lefts)
    return pl.pallas_call(
        partial(back_kernel, n, picks),
        grid=(depth // tile,),
        in_specs=[pl.BlockSpec((total, wide), lambda j: (0, 0))] * n
        + [pl.BlockSpec((tile, wide), lambda j: (j, 0))] * n,
        out_specs=[pl.BlockSpec((length, tile), lambda j: (0, j))] * len(picks),
        out_shape=[jax.ShapeDtypeStruct((length, depth), BF)] * len(picks),
        compiler_params=pltpu.CompilerParams(vmem_limit_bytes=44 << 20),
        cost_estimate=cost(2 * length * len(picks) * depth * wide * n / 6e8 + 1),
    )(*lefts, *weights)


def gated(sums, extras):
    gate, upward = sums
    grad = extras[0].astype(F32)
    inverse = 1.0 / (1.0 + jnp.exp(-gate))
    swish = gate * inverse
    return (
        swish * upward,
        grad * upward * (inverse + swish * (1.0 - inverse)),
        grad * swish,
    )


def after(value, *others):
    return lax.optimization_barrier((value,) + others)[0]


def after_all(values, *others):
    return lax.optimization_barrier(tuple(values) + others)[: len(values)]


def body(
    plan,
    tokens,
    segment_ids,
    cotangent,
    query_master,
    query_first,
    query_second,
    key_master,
    key_first,
    key_second,
    value_master,
    value_first,
    value_second,
    output_master,
    output_first,
    output_second,
    gate_master,
    gate_first,
    gate_second,
    up_master,
    up_first,
    up_second,
    down_master,
    down_first,
    down_second,
    norm_gains,
    gains_first,
    gains_second,
):
    inputs = plan.to_inner(tokens[0]).astype(F32)
    doc_start = segment_ids[0]
    length = inputs.shape[0]
    n_ctx = plan.shape["ctx"]
    ctx = lax.axis_index("ctx")
    rows = query_master.shape[0]
    gain_one = plan.to_inner(norm_gains[:D])
    gain_two = plan.to_inner(norm_gains[D : 2 * D])
    gain_query = norm_gains[2 * D : 2 * D + HD]
    gain_key = norm_gains[2 * D + HD :]

    attn_rows = jnp.concatenate(
        [
            part.astype(BF).reshape(rows, GROUP, -1)
            for part in (query_master, key_master, value_master, output_master)
        ],
        axis=2,
    ).reshape(rows, -1)
    attn_block = plan.weight_block(attn_rows)
    attn_cols = plan.weight_rows(attn_block)
    qkv_w = attn_cols[:, : QW + 2 * KW]
    out_w = attn_cols[:, QW + 2 * KW :]

    starts = jnp.concatenate(plan.gather_near(plan.gather_far(doc_start)), axis=0)
    total_len = starts.shape[0]
    spots = ctx * length + jnp.arange(length, dtype=jnp.int32)
    cosine, sine = rope_tables(jnp.tile(spots, GROUP) - starts)
    base = (ctx * length).astype(jnp.int32).reshape(1)
    starts_g = starts.reshape(GROUP, 1, length)
    head_gains = jnp.concatenate(
        [jnp.tile(gain_query, QW // HD), gain_key, jnp.ones((HD,), F32)]
    ).reshape(1, -1)
    normed_b = rms_scale(inputs, gain_one).astype(BF)
    normed_far = plan.gather_far(normed_b)
    down_block = plan.weight_block(after(down_master.astype(BF), attn_block, *normed_far))
    normed_list = plan.gather_near(after_all(normed_far, attn_cols, down_block))
    down_w = plan.weight_rows(down_block)
    qkv, normed_all = columns(normed_list, (qkv_w,), (), (F32,), lambda s, x: s, QW + 2 * KW)
    gate_block = plan.weight_block(after(gate_master.astype(BF), down_block))
    query_in, own_kv = prepare(qkv, cosine, sine, head_gains, length)
    own_kv = after(own_kv, gate_block)
    kv = [own_kv]
    for s in range(1, n_ctx):
        kv.append(lax.ppermute(kv[-1], "ctx", [(i, i + 1) for i in range(n_ctx - 1)]))
    up_block = plan.weight_block(after(up_master.astype(BF), kv[-1]))
    gate_w = plan.weight_rows(gate_block)
    up_w = plan.weight_rows(up_block)
    out_grad_b = plan.to_inner(cotangent[0])
    out_grad = out_grad_b.astype(F32)
    out_grad_far = plan.gather_far(after(out_grad_b, kv[-1]))
    attn_b, logs = flash_forward(base, starts_g, query_in, kv, length)

    out_grad_list = plan.gather_near(after_all(out_grad_far, logs))
    hidden_grad, out_grad_all = columns(out_grad_list, (down_w,), (), (BF,), lambda s, x: s, 512)
    middle = inputs + after(plan.scatter(back((after(attn_b, up_block),), (out_w,), 512)), hidden_grad)

    normed_two_b = rms_scale(middle, gain_two).astype(BF)
    two_list = plan.gather(normed_two_b)
    hidden_b, gate_grad_b, up_grad_b, two_all = columns(
        two_list, (gate_w, up_w), (hidden_grad,), (BF,) * 3, gated, 256
    )
    down_grad = across(out_grad_all, hidden_b).astype(BF)
    down_sum = plan.grad_sum(down_grad)
    gate_grad_b = after(gate_grad_b, down_grad)
    late, soon = (4, 2, 1, 0), (7, 6, 5, 3)
    two_soon = back((gate_grad_b, up_grad_b), (gate_w, up_w), 512, soon)
    two_late = back(
        (after(gate_grad_b, *two_soon), up_grad_b), (gate_w, up_w), 512, late
    )
    two_grad = dict(zip(soon + late, (*two_soon, *two_late)))
    gate_part = across(two_all, after(gate_grad_b, two_late[0])).astype(BF)
    up_part = across(two_all, after(up_grad_b, two_late[0])).astype(BF)
    out_blocks = back((after(hidden_b, two_late[0]),), (down_w,), 512)
    normed_two_grad = after(plan.scatter(two_grad), gate_part, up_part, out_blocks[0])
    gate_sum = plan.grad_sum(gate_part)
    _, norm_two_back = jax.vjp(rms_scale, middle, gain_two)
    middle_norm_grad, gain_two_grad = norm_two_back(normed_two_grad)
    middle_grad = out_grad + middle_norm_grad
    middle_grad_b = middle_grad.astype(BF)

    middle_list = plan.gather(middle_grad_b)
    attn_grad_b, middle_all = columns(middle_list, (out_w,), (), (BF,), lambda s, x: s, QW)
    branch = plan.scatter(after_all(out_blocks, attn_grad_b))
    result = middle + branch
    down_own = plan.grad_rows(after(down_sum, attn_grad_b))
    output_part = across(middle_all, attn_b).astype(BF)
    output_sum = plan.grad_sum(output_part)
    attn_grad_b = after(attn_grad_b, output_part)
    dquery, *dkv = flash_backward(base, starts_g, logs, query_in, attn_grad_b, kv, length)
    gate_own = plan.grad_rows(after(gate_sum, attn_grad_b))
    moving = dkv[-1]
    for s in range(n_ctx - 1, 0, -1):
        if s == 1:
            moving = after(moving, gate_own, result)
        moving = lax.ppermute(moving, "ctx", [(i + 1, i) for i in range(n_ctx - 1)])
        if s > 1:
            moving = (moving.astype(F32) + dkv[s - 1].astype(F32)).astype(BF)
        if s == n_ctx - 1:
            moving = after(moving, down_own)
    up_sum = plan.grad_sum(after(up_part, moving))
    output_own = plan.grad_rows(after(output_sum, dquery))
    dkv = (dkv[0], moving) if n_ctx > 1 else dkv
    qkv_grad_b, gain_heads = unprepare(after(qkv, output_own), cosine, sine, head_gains, dquery, dkv, length)
    gain_heads = gain_heads.reshape(-1, HD)
    gain_query_grad = jnp.sum(gain_heads[: QW // HD], axis=0)
    gain_key_grad = gain_heads[QW // HD]
    normed_grad = plan.scatter(back((qkv_grad_b,), (qkv_w,), 512))
    qkv_sum = plan.grad_sum(across(normed_all, qkv_grad_b).astype(BF))
    up_own = plan.grad_rows(after(up_sum, qkv_grad_b))
    normed_grad = after(normed_grad, up_own, output_own)
    _, norm_one_back = jax.vjp(rms_scale, inputs, gain_one)
    input_norm_grad, gain_one_grad = norm_one_back(normed_grad)
    input_grad = middle_grad + input_norm_grad

    sums = (down_sum, gate_sum, up_sum, output_sum, qkv_sum)
    squares = F32(0.0)
    for part in sums:
        wide = part.astype(F32)
        squares = squares + jnp.sum(wide * wide)
    gain_part = jnp.concatenate(
        [
            plan.to_outer(gain_one_grad),
            plan.to_outer(gain_two_grad),
            gain_query_grad,
            gain_key_grad,
            squares[None],
        ]
    )
    gain_total = plan.total(gain_part)
    square_total = gain_total[-1]
    gain_total = gain_total[:-1]
    qkv_own = plan.grad_rows(qkv_sum)
    qkv_own = qkv_own.reshape(rows, GROUP, -1)
    grad_norm = jnp.sqrt(square_total + jnp.sum(gain_total * gain_total))
    factor = jnp.minimum(1.0, clip_bound / (grad_norm + 1e-06))
    updated = [
        adam_update(
            weight,
            factor * grads.reshape(rows, -1).astype(F32),
            first,
            second,
            weight_rate,
            weight_decay,
        )
        for weight, first, second, grads in (
            (query_master, query_first, query_second, qkv_own[:, :, :QW]),
            (key_master, key_first, key_second, qkv_own[:, :, QW : QW + KW]),
            (value_master, value_first, value_second, qkv_own[:, :, QW + KW :]),
            (output_master, output_first, output_second, output_own),
            (gate_master, gate_first, gate_second, gate_own),
            (up_master, up_first, up_second, up_own),
            (down_master, down_first, down_second, down_own),
        )
    ]
    gains_done = adam_update(
        norm_gains, factor * gain_total, gains_first, gains_second, gain_rate, 0.0
    )
    return (
        plan.to_outer(result.astype(BF))[None],
        plan.to_outer(input_grad)[None],
        *(part for new in updated for part in new),
        *gains_done,
        grad_norm,
    )


def solution(mesh):
    plan = Plan(mesh)
    by_token = P(("dp", "fsdp"), "ctx", None)
    by_row = P(("dp", "ctx", "fsdp"), None)
    in_specs = (by_token, P(("dp", "fsdp"), "ctx"), by_token) + (by_row,) * 21 + (P(),) * 3
    out_specs = (by_token, by_token) + (by_row,) * 21 + (P(),) * 4
    return jax.shard_map(
        partial(body, plan), mesh=mesh, in_specs=in_specs, out_specs=out_specs, check_vma=False
    )
```

```python
from functools import partial

import jax
import jax.numpy as jnp
from jax import lax
from jax.experimental import pallas as pl
from jax.experimental.pallas import tpu as pltpu
from jax.sharding import PartitionSpec as P

D = 2048
H = 32
HD = 64
KVH = 8
FF = 8192
STEP = 10


eps_norm = 1e-05
rope_base = 1000000.0
clip_bound = 1.0
beta_one = 0.9
beta_two = 0.95
adam_eps = 1e-08
weight_decay = 0.1
weight_rate = 0.04
gain_rate = 0.4
masked = -1e30

BF = jnp.bfloat16
F32 = jnp.float32
GROUP = KVH
QW = H * HD // GROUP
KW = HD
FW = FF // GROUP


class Plan:
    def __init__(self, mesh):
        shape = dict(mesh.shape)
        self.shape = shape
        if shape["dp"] * shape["fsdp"] == GROUP:
            self.tp = ("dp", "fsdp")
        elif shape["dp"] == GROUP:
            self.tp = ("dp",)
        elif shape["fsdp"] == GROUP:
            self.tp = ("fsdp",)
        else:
            raise ValueError("unsupported mesh")
        self.rest = tuple(a for a in ("ctx", "dp", "fsdp") if a not in self.tp)
        self.all = ("dp", "ctx", "fsdp")
        self.two_by_four = self.tp == ("dp", "fsdp") and shape["dp"] == 2

    def me(self):
        return lax.axis_index(self.tp)

    def swap(self, value, bits):
        return lax.ppermute(value, self.tp, [(i, i ^ bits) for i in range(GROUP)])

    def to_inner(self, value):
        lead = value.shape[:-1]
        sizes = [self.shape[a] for a in self.all]
        n = len(lead)
        shaped = value.reshape(*lead, *sizes, -1)
        order = [n + self.all.index(a) for a in self.rest + self.tp]
        return shaped.transpose(*range(n), *order, n + 3).reshape(value.shape)

    def to_outer(self, value):
        lead = value.shape[:-1]
        names = self.rest + self.tp
        sizes = [self.shape[a] for a in names]
        n = len(lead)
        shaped = value.reshape(*lead, *sizes, -1)
        order = [n + names.index(a) for a in self.all]
        return shaped.transpose(*range(n), *order, n + 3).reshape(value.shape)

    def gather_one(self, own):
        if not self.two_by_four:
            return [own] + [self.swap(own, r) for r in range(1, GROUP)]
        return [own, self.swap(own, 2), self.swap(own, 4)]

    def gather_two(self, held):
        if not self.two_by_four:
            return held
        own, by_y, by_x = held
        half = own.shape[0] // 2
        corner = [self.swap(by_y[:half], 4), self.swap(by_x[half:], 2)]
        return [own, self.swap(own, 1), by_y, self.swap(by_y, 1), by_x, *corner]

    def gather_three(self, held):
        if not self.two_by_four:
            return held
        by_x, *corner = held[4:]
        return held[:5] + [self.swap(by_x, 1)] + corner + [self.swap(part, 1) for part in corner]

    def scatter_one(self, blocks):
        if not self.two_by_four:
            return [blocks[0]] + [self.swap(blocks[r], r) for r in range(1, GROUP)]
        return [(blocks[r], self.swap(blocks[r + 1], 1)) for r in range(0, len(blocks), 2)]

    def scatter_two(self, held):
        if not self.two_by_four:
            return held
        own, by_y, by_x, corner = [left.astype(F32) + right.astype(F32) for left, right in held]
        corner = corner.astype(BF)
        half = corner.shape[0] // 2
        return [own, by_y, by_x, self.swap(corner[:half], 4), self.swap(corner[half:], 2)]

    def scatter_three(self, held):
        if not self.two_by_four:
            return held
        own, by_y, by_x, top, low = held
        half = top.shape[0]
        by_y = jnp.concatenate([by_y[:half] + top.astype(F32), by_y[half:]], axis=0).astype(BF)
        by_x = jnp.concatenate([by_x[:half], by_x[half:] + low.astype(F32)], axis=0).astype(BF)
        return [own, self.swap(by_y, 2), self.swap(by_x, 4)]

    def scatter_end(self, held):
        total = held[0].astype(F32)
        for part in held[1:]:
            total = total + part.astype(F32)
        return total

    def exchange(self, pick):
        me = self.me()
        return [pick(me)] + [self.swap(pick(me ^ r), r) for r in range(1, GROUP)]

    def weight_block(self, parts, *firsts):
        def pick(p):
            cut = []
            for part in parts:
                width = part.shape[1] // GROUP
                cut.append(lax.dynamic_slice_in_dim(part, p * width, width, 1))
            return cut[0] if len(cut) == 1 else jnp.concatenate(cut, axis=1)

        (stacked,) = place(self.me().reshape(1), [after_all(self.exchange(pick), *firsts)], ())
        return stacked.reshape(-1, stacked.shape[-1])

    def weight_rows(self, block):
        return lax.all_gather(block, self.rest, axis=0, tiled=True)

    def grad_sum(self, grad):
        mine = lax.psum_scatter(grad, self.rest, scatter_dimension=0, tiled=True)
        return mine.reshape(GROUP, -1, grad.shape[1])

    def grad_parts(self, mines):
        def pick(p):
            cut = [lax.dynamic_index_in_dim(mine, p, 0, keepdims=False) for mine in mines]
            return cut[0] if len(cut) == 1 else jnp.concatenate(cut, axis=1)

        return self.exchange(pick)

    def grad_rows(self, mines, cuts, *firsts):
        return self.grad_placed(after_all(self.grad_parts(mines), *firsts), cuts)

    def grad_placed(self, got, cuts):
        outs = [[(0, first, width)] for first, width in cuts]
        return place(self.me().reshape(1), [got], outs)

    def total(self, value, beside):
        size = 1
        for axis in self.all:
            size *= self.shape[axis]

        def other(bits):
            return lax.ppermute(value, self.all, [(i, i ^ bits) for i in range(size)])

        step = 1
        while step < size:
            if 2 * step < size:
                value = (value + other(step)) + (other(2 * step) + other(3 * step))
            else:
                value = value + other(step)
            if step == 1:
                value, beside = together(value, beside)
            step *= 4
        return value, beside


def rms_scale(values, gain):
    return values * lax.rsqrt(jnp.mean(values * values, axis=-1, keepdims=True) + eps_norm) * gain


def rope_tables(positions):
    half = HD // 2
    freq = rope_base ** (-(jnp.arange(half, dtype=jnp.float32) * 2.0 / HD))
    angle = positions.astype(jnp.float32)[:, None] * freq[None, :]
    cosine, sine = jnp.cos(angle), jnp.sin(angle)
    return (
        jnp.concatenate([cosine] * 4, axis=1),
        jnp.concatenate([-sine, sine, -sine, sine], axis=1),
    )


def across(left, right):
    return lax.dot_general(
        left, right, (((0,), (0,)), ((), ())), preferred_element_type=jnp.float32
    )


def against(left, right):
    return lax.dot_general(
        left, right, (((1,), (1,)), ((), ())), preferred_element_type=jnp.float32
    )


def plain(left, right):
    return jnp.dot(left, right, preferred_element_type=jnp.float32)


def adam_update(weight, grad, first, second, rate, decay):
    first_new = beta_one * first + (1.0 - beta_one) * grad
    second_new = beta_two * second + (1.0 - beta_two) * grad * grad
    ratio = (
        first_new
        / (1.0 - beta_one**STEP)
        / (jnp.sqrt(second_new / (1.0 - beta_two**STEP)) + adam_eps)
    )
    return (first_new, second_new, weight - rate * (ratio + decay * weight))


LANES = 2 * HD


def cost(time):
    return pl.CostEstimate(flops=int(time * 1e9), bytes_accessed=1, transcendentals=0)


def swap_halves(values):
    width = values.shape[-1]
    lane = lax.broadcasted_iota(jnp.int32, values.shape, 1)
    ahead = pltpu.roll(values, width - HD // 2, 1)
    behind = pltpu.roll(values, HD // 2, 1)
    return jnp.where(lane % HD < HD // 2, ahead, behind)


def by_head(values):
    width = values.shape[1]
    row = lax.broadcasted_iota(jnp.int32, (width, width), 0)
    col = lax.broadcasted_iota(jnp.int32, (width, width), 1)
    same = jnp.where(row // HD == col // HD, 1.0 / HD, 0.0).astype(BF)
    high = values.astype(BF)
    low = (values - high.astype(F32)).astype(BF)
    return jnp.dot(high, same, preferred_element_type=F32) + jnp.dot(
        low, same, preferred_element_type=F32
    )


def prepare_kernel(raw_ref, cos_ref, sin_ref, gain_ref, query_ref, kv_ref):
    raw = raw_ref[...]
    heads = raw.shape[1] // HD
    cosine = jnp.concatenate([cos_ref[...]] * (heads // 2), axis=1)
    sine = jnp.concatenate([sin_ref[...]] * (heads // 2), axis=1)
    normed = raw * lax.rsqrt(by_head(raw * raw) + eps_norm) * gain_ref[...]
    turned = normed * cosine + swap_halves(normed) * sine
    query_ref[...] = turned[:, :QW].astype(BF)
    tail = turned[:, QW:]
    lane = lax.broadcasted_iota(jnp.int32, tail.shape, 1)
    kv_ref[...] = jnp.where(lane < KW, tail, raw[:, QW:]).astype(BF)


def prepare(raw, cosine, sine, gains, tile):
    total, width = raw.shape
    return pl.pallas_call(
        prepare_kernel,
        grid=(total // tile,),
        in_specs=[
            pl.BlockSpec((tile, width), lambda i: (i, 0)),
            pl.BlockSpec((tile, LANES), lambda i: (i, 0)),
            pl.BlockSpec((tile, LANES), lambda i: (i, 0)),
            pl.BlockSpec((1, width), lambda i: (0, 0)),
        ],
        out_specs=[
            pl.BlockSpec((tile, QW), lambda i: (i, 0)),
            pl.BlockSpec((tile, LANES), lambda i: (i, 0)),
        ],
        out_shape=[
            jax.ShapeDtypeStruct((total, QW), BF),
            jax.ShapeDtypeStruct((total, LANES), BF),
        ],
        compiler_params=pltpu.CompilerParams(vmem_limit_bytes=24 << 20),
        cost_estimate=cost(6),
    )(raw, cosine, sine, gains)


def unprepare_kernel(n_ctx, raw_ref, cos_ref, sin_ref, gain_ref, dq_ref, *refs):
    parts, (out_ref, dgain_ref) = refs[:n_ctx], refs[n_ctx:]
    raw = raw_ref[...]
    heads = raw.shape[1] // HD
    cosine = jnp.concatenate([cos_ref[...]] * (heads // 2), axis=1)
    sine = jnp.concatenate([sin_ref[...]] * (heads // 2), axis=1)
    gain = gain_ref[...]
    dkv = parts[0][...]
    for part in parts[1:]:
        dkv = dkv + part[...].astype(F32)
    upper = jnp.concatenate([dq_ref[...], dkv], axis=1)
    dnormed = upper * cosine + swap_halves(upper * sine)
    scale = lax.rsqrt(by_head(raw * raw) + eps_norm)
    dgain = dnormed * raw * scale
    inner = dnormed * gain
    draw = scale * inner - raw * (scale * scale * scale) * by_head(inner * raw)
    lane = lax.broadcasted_iota(jnp.int32, upper.shape, 1)
    out_ref[...] = jnp.where(lane < QW + KW, draw, upper).astype(BF)
    total = jnp.sum(dgain, axis=0, keepdims=True)

    @pl.when(pl.program_id(0) == 0)
    def _():
        dgain_ref[...] = total

    @pl.when(pl.program_id(0) > 0)
    def _():
        dgain_ref[...] += total


def unprepare(raw, cosine, sine, gains, dquery, dkv, tile):
    total, width = raw.shape
    kv_spec = pl.BlockSpec((tile, LANES), lambda i: (i, 0))
    return pl.pallas_call(
        partial(unprepare_kernel, len(dkv)),
        grid=(total // tile,),
        in_specs=[
            pl.BlockSpec((tile, width), lambda i: (i, 0)),
            kv_spec,
            kv_spec,
            pl.BlockSpec((1, width), lambda i: (0, 0)),
            pl.BlockSpec((tile, QW), lambda i: (i, 0)),
        ]
        + [kv_spec] * len(dkv),
        out_specs=[
            pl.BlockSpec((tile, width), lambda i: (i, 0)),
            pl.BlockSpec((1, width), lambda i: (0, 0)),
        ],
        out_shape=[
            jax.ShapeDtypeStruct((total, width), BF),
            jax.ShapeDtypeStruct((1, width), F32),
        ],
        compiler_params=pltpu.CompilerParams(vmem_limit_bytes=24 << 20),
        cost_estimate=cost(11),
    )(raw, cosine, sine, gains, dquery, *dkv)


def allowed_bias(base, start, n_ctx, length):
    shape = (n_ctx * length, length)
    key = lax.broadcasted_iota(jnp.int32, shape, 0)
    key_place = base + key % length - (key // length) * length
    place = base + lax.broadcasted_iota(jnp.int32, shape, 1)
    return jnp.where((key_place >= start) & (key_place <= place), 0.0, masked)


def by_rows(left, right):
    return lax.dot_general(
        left, right, (((1,), (1,)), ((), ())), preferred_element_type=jnp.float32
    )


def flash_forward_kernel(n_ctx, base_ref, start_ref, query_ref, *refs):
    kv_refs, (out_ref, log_ref) = refs[:n_ctx], refs[n_ctx:]
    length = query_ref.shape[0]
    kv = jnp.concatenate([ref[...] for ref in kv_refs], axis=0)
    keys, values = kv[:, :HD], kv[:, HD:]
    values_t = values.T
    bias = allowed_bias(base_ref[0], start_ref[0], n_ctx, length)
    outs, logs = [], []
    for head in range(QW // HD):
        query = query_ref[:, head * HD : (head + 1) * HD] * BF(HD**-0.5)
        scores = by_rows(keys, query) + bias
        top = jnp.max(scores, axis=0, keepdims=True)
        weights = jnp.exp(scores - top)
        total = jnp.sum(weights, axis=0, keepdims=True)
        probs = (weights * (1.0 / total)).astype(BF)
        outs.append(jnp.dot(values_t, probs, preferred_element_type=F32))
        logs.append(top + jnp.log(total))
    out_ref[...] = jnp.concatenate(outs, axis=0).T.astype(BF)
    log_ref[0] = jnp.concatenate(logs, axis=0)


def flash_forward(base, starts, query, kv, length):
    total = query.shape[0]
    blocks = total // length
    heads = QW // HD
    n_ctx = len(kv)
    return pl.pallas_call(
        partial(flash_forward_kernel, n_ctx),
        grid=(blocks,),
        in_specs=[
            pl.BlockSpec(memory_space=pltpu.SMEM),
            pl.BlockSpec((1, 1, length), lambda i: (i, 0, 0)),
            pl.BlockSpec((length, QW), lambda i: (i, 0)),
        ]
        + [pl.BlockSpec((length, LANES), lambda i: (i, 0))] * n_ctx,
        out_specs=[
            pl.BlockSpec((length, QW), lambda i: (i, 0)),
            pl.BlockSpec((1, heads, length), lambda i: (i, 0, 0)),
        ],
        out_shape=[
            jax.ShapeDtypeStruct((total, QW), BF),
            jax.ShapeDtypeStruct((blocks, heads, length), F32),
        ],
        compiler_params=pltpu.CompilerParams(vmem_limit_bytes=40 << 20),
        cost_estimate=cost(28),
    )(base, starts, query, *kv)


def flash_backward_kernel(n_ctx, base_ref, start_ref, log_ref, query_ref, upper_ref, *refs):
    kv_refs, dq_ref, dkv_refs = refs[:n_ctx], refs[n_ctx], refs[n_ctx + 1 :]
    length = query_ref.shape[0]
    kv = jnp.concatenate([ref[...] for ref in kv_refs], axis=0)
    keys, values = kv[:, :HD], kv[:, HD:]
    keys_t = keys.T
    bias = allowed_bias(base_ref[0], start_ref[0], n_ctx, length)
    dqs = []
    dkeys = dvalues = None
    for head in range(QW // HD):
        cols = slice(head * HD, (head + 1) * HD)
        query = query_ref[:, cols] * BF(HD**-0.5)
        upper = upper_ref[:, cols]
        scores = by_rows(keys, query) + bias
        probs = jnp.exp(scores - log_ref[0, head : head + 1, :])
        dprobs = by_rows(values, upper)
        delta = jnp.sum(probs * dprobs, axis=0, keepdims=True)
        dscores = (probs * (dprobs - delta)).astype(BF)
        dqs.append(jnp.dot(keys_t, dscores, preferred_element_type=F32) * HD**-0.5)
        dkey = jnp.dot(dscores, query, preferred_element_type=F32)
        dvalue = jnp.dot(probs.astype(BF), upper, preferred_element_type=F32)
        dkeys = dkey if dkeys is None else dkeys + dkey
        dvalues = dvalue if dvalues is None else dvalues + dvalue
    dq_ref[...] = jnp.concatenate(dqs, axis=0).T
    dkv = jnp.concatenate([dkeys, dvalues], axis=1)
    for s in range(n_ctx):
        dkv_refs[s][...] = dkv[s * length : (s + 1) * length].astype(dkv_refs[s].dtype)


def flash_backward(base, starts, logs, query, upper, kv, length):
    total = query.shape[0]
    blocks = total // length
    heads = QW // HD
    n_ctx = len(kv)
    kv_spec = pl.BlockSpec((length, LANES), lambda i: (i, 0))
    q_spec = pl.BlockSpec((length, QW), lambda i: (i, 0))
    return pl.pallas_call(
        partial(flash_backward_kernel, n_ctx),
        grid=(blocks,),
        in_specs=[
            pl.BlockSpec(memory_space=pltpu.SMEM),
            pl.BlockSpec((1, 1, length), lambda i: (i, 0, 0)),
            pl.BlockSpec((1, heads, length), lambda i: (i, 0, 0)),
            q_spec,
            q_spec,
        ]
        + [kv_spec] * n_ctx,
        out_specs=[q_spec] + [kv_spec] * n_ctx,
        out_shape=[jax.ShapeDtypeStruct((total, QW), F32)]
        + [jax.ShapeDtypeStruct((total, LANES), BF if s else F32) for s in range(n_ctx)],
        compiler_params=pltpu.CompilerParams(vmem_limit_bytes=48 << 20),
        cost_estimate=cost(35),
    )(base, starts, logs, query, upper, *kv)


def place_kernel(n, outs, me_ref, *refs):
    lists = [refs[i * GROUP : (i + 1) * GROUP] for i in range(n)]
    out_refs = refs[n * GROUP :]
    for r in range(GROUP):
        owner = me_ref[0] ^ r
        if not outs:
            out_refs[0][owner] = lists[0][r][...]
        for out_ref, cuts in zip(out_refs, outs):
            wide = sum(width for _, _, width in cuts)
            at = 0
            for i, first, width in cuts:
                start = pl.multiple_of(owner * wide + at, LANES)
                out_ref[:, pl.ds(start, width)] = lists[i][r][:, first : first + width]
                at += width


def place(me, lists, outs):
    rows, width = lists[0][0].shape
    if outs:
        shapes = [(rows, GROUP * sum(width for _, _, width in cuts)) for cuts in outs]
    else:
        shapes = [(GROUP, rows, width)]
    return pl.pallas_call(
        partial(place_kernel, len(lists), outs),
        in_specs=[pl.BlockSpec(memory_space=pltpu.SMEM)]
        + [pl.BlockSpec(memory_space=pltpu.VMEM)] * (GROUP * len(lists)),
        out_specs=[pl.BlockSpec(memory_space=pltpu.VMEM)] * len(shapes),
        out_shape=[jax.ShapeDtypeStruct(shape, lists[0][0].dtype) for shape in shapes],
        cost_estimate=cost(2),
    )(me, *[block for one in lists for block in one])


def columns_kernel(epilogue, n_b, cuts, n_x, *refs):
    blocks, refs = refs[:n_b], refs[n_b:]
    weights, refs = refs[: len(cuts)], refs[len(cuts) :]
    extras, refs = refs[:n_x], refs[n_x:]
    outs, (held, sems) = refs[:-2], refs[-2:]
    chunk = held.shape[0] // 4

    @pl.when(pl.program_id(0) == 0)
    def _():
        copies, start = [], 0
        for r, block in enumerate(blocks):
            there = held.at[pl.ds(start, block.shape[0])]
            copies.append(pltpu.make_async_copy(block, there, sems.at[r]))
            start += block.shape[0]
        for copy in copies:
            copy.start()
        for copy in copies:
            copy.wait()

    @pl.loop(0, 4)
    def _(r):
        rows = pl.ds(pl.multiple_of(r * chunk, chunk), chunk)
        left = held[rows, :]
        sums = [
            jnp.dot(left, w[:, cut], preferred_element_type=F32) for w, cut in zip(weights, cuts)
        ]
        for out, value in zip(outs, epilogue(sums, [x[rows, :] for x in extras])):
            out[rows, :] = value.astype(out.dtype)


def weight_spec(weight, tile, rows):
    array, first, width = weight
    if first % tile:
        return pl.BlockSpec((rows, array.shape[1]), lambda j: (0, 0)), slice(first, first + width)
    return pl.BlockSpec((rows, tile), lambda j: (0, first // tile + j)), slice(0, tile)


def columns(blocks, weights, extras, outs, epilogue, tile):
    n_b = len(blocks)
    depth = blocks[0].shape[1]
    total = sum(block.shape[0] for block in blocks)
    wide = weights[0][2]
    by_tile = pl.BlockSpec((total, tile), lambda j: (0, j))
    specs = [weight_spec(w, tile, depth) for w in weights]
    return pl.pallas_call(
        partial(columns_kernel, epilogue, n_b, [cut for _, cut in specs], len(extras)),
        grid=(wide // tile,),
        in_specs=[pl.BlockSpec(memory_space=pl.ANY)] * n_b
        + [spec for spec, _ in specs]
        + [by_tile] * len(extras),
        out_specs=[by_tile] * len(outs) + [pl.BlockSpec((total, depth), lambda j: (0, 0))],
        out_shape=[jax.ShapeDtypeStruct((total, wide), kind) for kind in outs]
        + [jax.ShapeDtypeStruct((total, depth), BF)],
        scratch_shapes=[pltpu.SemaphoreType.DMA((n_b,))],
        compiler_params=pltpu.CompilerParams(vmem_limit_bytes=52 << 20),
        cost_estimate=cost(2 * total * depth * wide * len(weights) / 6e8 + 3),
    )(*blocks, *[w[0] for w in weights], *extras)


def summed_kernel(left_ref, right_ref, out_ref):
    out_ref[...] = across(left_ref[...], right_ref[...]).astype(BF)


def summed(left, right, tile=512):
    total, depth = left.shape
    wide = right.shape[1]
    return pl.pallas_call(
        summed_kernel,
        grid=(depth // tile,),
        in_specs=[
            pl.BlockSpec((total, tile), lambda j: (0, j)),
            pl.BlockSpec((total, wide), lambda j: (0, 0)),
        ],
        out_specs=pl.BlockSpec((tile, wide), lambda j: (j, 0)),
        out_shape=jax.ShapeDtypeStruct((depth, wide), BF),
        compiler_params=pltpu.CompilerParams(vmem_limit_bytes=44 << 20),
        cost_estimate=cost(2 * total * depth * wide / 6e8 + 1),
    )(left, right)


def back_kernel(n, cuts, picks, *refs):
    lefts, weights, outs = refs[:n], refs[n : 2 * n], refs[2 * n :]
    length = outs[0].shape[0]
    for r, out in zip(picks, outs):
        rows = slice(r * length, (r + 1) * length)
        total = by_rows(lefts[0][rows, :], weights[0][:, cuts[0]])
        for left, weight, cut in zip(lefts[1:], weights[1:], cuts[1:]):
            total = total + by_rows(left[rows, :], weight[:, cut])
        out[...] = total.astype(BF)


def back(lefts, weights, tile, picks=tuple(range(GROUP))):
    total, wide = lefts[0].shape
    depth = weights[0][0].shape[0]
    length = total // GROUP
    n = len(lefts)
    specs, cuts = [], []
    for array, first, width in weights:
        if first % width:
            specs.append(pl.BlockSpec((tile, array.shape[1]), lambda j: (j, 0)))
            cuts.append(slice(first, first + width))
        else:
            specs.append(pl.BlockSpec((tile, width), lambda j, at=first // width: (j, at)))
            cuts.append(slice(0, width))
    return pl.pallas_call(
        partial(back_kernel, n, cuts, picks),
        grid=(depth // tile,),
        in_specs=[pl.BlockSpec((total, wide), lambda j: (0, 0))] * n + specs,
        out_specs=[pl.BlockSpec((length, tile), lambda j: (0, j))] * len(picks),
        out_shape=[jax.ShapeDtypeStruct((length, depth), BF)] * len(picks),
        compiler_params=pltpu.CompilerParams(vmem_limit_bytes=44 << 20),
        cost_estimate=cost(2 * length * len(picks) * depth * wide * n / 6e8 + 1),
    )(*lefts, *[w[0] for w in weights])


def gated(sums, extras):
    gate, upward = sums
    grad = extras[0].astype(F32)
    inverse = 1.0 / (1.0 + jnp.exp(-gate))
    swish = gate * inverse
    return (
        swish * upward,
        grad * upward * (inverse + swish * (1.0 - inverse)),
        grad * swish,
    )


def after(value, *others):
    return lax.optimization_barrier((value,) + others)[0]


def together(*values):
    return lax.optimization_barrier(values)


def after_all(values, *others):
    return lax.optimization_barrier(tuple(values) + others)[: len(values)]


def body(
    plan,
    tokens,
    segment_ids,
    cotangent,
    query_master,
    query_first,
    query_second,
    key_master,
    key_first,
    key_second,
    value_master,
    value_first,
    value_second,
    output_master,
    output_first,
    output_second,
    gate_master,
    gate_first,
    gate_second,
    up_master,
    up_first,
    up_second,
    down_master,
    down_first,
    down_second,
    norm_gains,
    gains_first,
    gains_second,
):
    inputs = plan.to_inner(tokens[0]).astype(F32)
    doc_start = segment_ids[0]
    length = inputs.shape[0]
    n_ctx = plan.shape["ctx"]
    ctx = lax.axis_index("ctx")
    rows = query_master.shape[0]
    gain_one = plan.to_inner(norm_gains[:D])
    gain_two = plan.to_inner(norm_gains[D : 2 * D])
    gain_query = norm_gains[2 * D : 2 * D + HD]
    gain_key = norm_gains[2 * D + HD :]

    attn_rows = jnp.concatenate(
        [
            part.astype(BF).reshape(rows, GROUP, -1)
            for part in (query_master, key_master, value_master, output_master)
        ],
        axis=2,
    ).reshape(rows, -1)
    starts, step = doc_start, 1
    while step < GROUP:
        starts = jnp.concatenate([starts, plan.swap(starts, step)])
        step *= 2
    total_len = starts.shape[0]
    spots = ctx * length + jnp.arange(length, dtype=jnp.int32)
    cosine, sine = rope_tables(jnp.tile(spots, GROUP) - starts)
    base = (ctx * length).astype(jnp.int32).reshape(1)
    starts_g = starts.reshape(GROUP, 1, length)
    head_gains = jnp.concatenate(
        [jnp.tile(gain_query, QW // HD), gain_key, jnp.ones((HD,), F32)]
    ).reshape(1, -1)
    normed_b = rms_scale(inputs, gain_one).astype(BF)
    out_grad_b = plan.to_inner(cotangent[0])
    down_low, gate_low, up_low = [w.astype(BF) for w in (down_master, gate_master, up_master)]

    attn_block = plan.weight_block([attn_rows])
    attn_block, normed_b, down_low, out_grad_b = together(
        attn_block, normed_b, down_low, out_grad_b
    )
    attn_cols = plan.weight_rows(attn_block)
    held = plan.gather_one(normed_b)
    down_block = plan.weight_block([down_low])
    held, down_block, cosine, sine = together(held, down_block, cosine, sine)
    down_all = plan.weight_rows(down_block)
    held = plan.gather_two(held)
    held, gate_low, up_low, attn_cols = together(held, gate_low, up_low, attn_cols)
    qkv_w = (attn_cols, 0, QW + 2 * KW)
    out_w = (attn_cols, QW + 2 * KW, QW)
    normed_list = plan.gather_three(held)
    qkv, normed_all = columns(normed_list, (qkv_w,), (), (F32,), lambda s, x: s, QW + 2 * KW)
    query_in, own_kv = prepare(qkv, cosine, sine, head_gains, length)

    wide_block = plan.weight_block([gate_low, up_low], own_kv)
    query_in, own_kv, wide_block, out_grad_b = together(query_in, own_kv, wide_block, out_grad_b)
    kv = [own_kv] + [
        lax.ppermute(own_kv, "ctx", [(i, i + s) for i in range(n_ctx - s)])
        for s in range(1, n_ctx)
    ]
    held = plan.gather_one(out_grad_b)
    kv, held, down_all, wide_block = together(kv, held, down_all, wide_block)
    wide_all = plan.weight_rows(wide_block)
    held = plan.gather_two(held)
    attn_b, logs = flash_forward(base, starts_g, query_in, kv, length)
    attn_b, held = together(attn_b, held)
    gate_w, up_w, down_w = (wide_all, 0, FW), (wide_all, FW, FW), (down_all, 0, FW)
    out_grad_list = plan.gather_three(held)
    blocks = back((attn_b,), (out_w,), 512)
    blocks, out_grad_list = together(blocks, out_grad_list)
    held = plan.scatter_one(blocks)
    held = together(*held)
    held = plan.scatter_two(held)
    held, out_grad_list = together(held, out_grad_list)
    held = plan.scatter_three(held)
    hidden_grad, out_grad_all = columns(out_grad_list, (down_w,), (), (BF,), lambda s, x: s, 512)
    held, hidden_grad, out_grad_all = together(held, hidden_grad, out_grad_all)
    middle = inputs + plan.scatter_end(held)

    normed_two_b = rms_scale(middle, gain_two).astype(BF)
    held = together(*plan.gather_one(normed_two_b))
    held = together(*plan.gather_two(list(held)))
    two_list = plan.gather_three(list(held))
    hidden_b, gate_grad_b, up_grad_b, two_all = columns(
        two_list, (gate_w, up_w), (hidden_grad,), (BF,) * 3, gated, 256
    )
    down_part = summed(out_grad_all, hidden_b)
    gate_grad_b, up_grad_b, hidden_b, two_all, down_part = together(
        gate_grad_b, up_grad_b, hidden_b, two_all, down_part
    )
    down_sum = plan.grad_sum(down_part)
    soon = back((gate_grad_b, up_grad_b), (gate_w, up_w), 512, (7, 6, 5, 4))
    soon, gate_grad_b, up_grad_b, hidden_b = together(soon, gate_grad_b, up_grad_b, hidden_b)
    held_b = plan.scatter_one(list(soon)[::-1]) if plan.two_by_four else list(soon)[::-1]
    late = back((gate_grad_b, up_grad_b), (gate_w, up_w), 512, (3, 2, 1, 0))
    held_b, late, hidden_b, gate_grad_b = together(held_b, late, hidden_b, gate_grad_b)
    if plan.two_by_four:
        held = plan.scatter_two(plan.scatter_one(list(late)[::-1]) + list(held_b))
    else:
        held = plan.scatter_one(list(late)[::-1] + list(held_b))
    gate_part = summed(two_all, gate_grad_b)
    held, gate_part, up_grad_b = together(held, gate_part, up_grad_b)
    gate_sum = plan.grad_sum(gate_part)
    held = plan.scatter_three(held)
    up_part = summed(two_all, up_grad_b)
    held, up_part, hidden_b = together(held, up_part, hidden_b)
    normed_two_grad = plan.scatter_end(held)
    _, norm_two_back = jax.vjp(rms_scale, middle, gain_two)
    middle_norm_grad, gain_two_grad = norm_two_back(normed_two_grad)
    middle_grad = out_grad_b.astype(F32) + middle_norm_grad
    middle_grad_b = middle_grad.astype(BF)

    middle_grad_b, hidden_b = together(middle_grad_b, hidden_b)
    held = plan.gather_one(middle_grad_b)
    blocks = back((hidden_b,), (down_w,), 512)
    held, blocks = together(held, blocks)
    held = plan.gather_two(held)
    out_held = plan.scatter_one(blocks)
    held, out_held = together(held, out_held)
    middle_list = plan.gather_three(held)
    attn_grad_b, middle_all = columns(middle_list, (out_w,), (), (BF,), lambda s, x: s, QW)
    output_part = summed(middle_all, attn_b)
    attn_grad_b, output_part, out_held, down_sum, gate_sum = together(
        attn_grad_b, output_part, out_held, down_sum, gate_sum
    )
    output_sum = plan.grad_sum(output_part)
    up_sum = plan.grad_sum(up_part)
    out_held = plan.scatter_two(out_held)
    dquery, *dkv = flash_backward(base, starts_g, logs, query_in, attn_grad_b, kv, length)
    dkv = [dkv[0]] + [
        lax.ppermute(dkv[s], "ctx", [(i + s, i) for i in range(n_ctx - s)])
        for s in range(1, n_ctx)
    ]
    out_held = plan.scatter_three(after_all(out_held, dquery))
    sums = after_all((gate_sum, down_sum), dquery)
    gate_own, down_own = plan.grad_rows(sums, [(0, FW), (FW, FW)], *dkv)
    dkv, out_held, gate_own, down_own = together(dkv, out_held, gate_own, down_own)
    qkv_grad_b, gain_heads = unprepare(qkv, cosine, sine, head_gains, dquery, dkv, length)
    gain_heads = gain_heads.reshape(-1, HD)
    gain_query_grad = jnp.sum(gain_heads[: QW // HD], axis=0)
    gain_key_grad = gain_heads[QW // HD]
    blocks = back((qkv_grad_b,), (qkv_w,), 512)
    blocks, qkv_grad_b, output_sum, up_sum = together(blocks, qkv_grad_b, output_sum, up_sum)
    held = plan.scatter_one(blocks)
    qkv_part = summed(normed_all, qkv_grad_b)
    held, qkv_part = together(held, qkv_part)
    qkv_sum = plan.grad_sum(qkv_part)
    held = plan.scatter_two(held)
    held = together(*held)
    result = middle + plan.scatter_end(out_held)
    held = plan.scatter_three(list(held))
    squares = F32(0.0)
    for part in (down_sum, gate_sum, up_sum, output_sum):
        wide = part.astype(F32)
        squares = squares + jnp.sum(wide * wide)
    result = plan.to_outer(result.astype(BF))
    held, squares, result, qkv_sum = together(held, squares, result, qkv_sum)
    normed_grad = plan.scatter_end(held)
    _, norm_one_back = jax.vjp(rms_scale, inputs, gain_one)
    input_norm_grad, gain_one_grad = norm_one_back(normed_grad)
    input_grad = middle_grad + input_norm_grad

    gain_one_grad, gain_two_grad = plan.to_outer(gain_one_grad), plan.to_outer(gain_two_grad)
    qkv_sum, squares, gain_one_grad, gain_two_grad = together(
        qkv_sum, squares, gain_one_grad, gain_two_grad
    )
    wide = qkv_sum.astype(F32)
    squares = squares + jnp.sum(wide * wide)
    gain_part = jnp.concatenate(
        [
            gain_one_grad,
            gain_two_grad,
            gain_query_grad,
            gain_key_grad,
            squares[None],
        ]
    )
    parts = plan.grad_parts((qkv_sum, output_sum, up_sum))
    gain_total, (parts, input_grad) = plan.total(gain_part, (parts, plan.to_outer(input_grad)))
    square_total = gain_total[-1]
    gain_total = gain_total[:-1]
    at = QW + 2 * KW
    query_own, kv_own, output_own, up_own = plan.grad_placed(
        parts, [(0, QW), (QW, 2 * KW), (at, QW), (at + QW, FW)]
    )
    kv_own = kv_own.reshape(rows, GROUP, -1)
    key_own, value_own = [kv_own[:, :, at : at + KW].reshape(rows, -1) for at in (0, KW)]
    grad_norm = jnp.sqrt(square_total + jnp.sum(gain_total * gain_total))
    factor = jnp.minimum(1.0, clip_bound / (grad_norm + 1e-06))
    updated = [
        adam_update(
            weight,
            factor * grads.astype(F32),
            first,
            second,
            weight_rate,
            weight_decay,
        )
        for weight, first, second, grads in (
            (query_master, query_first, query_second, query_own),
            (key_master, key_first, key_second, key_own),
            (value_master, value_first, value_second, value_own),
            (output_master, output_first, output_second, output_own),
            (gate_master, gate_first, gate_second, gate_own),
            (up_master, up_first, up_second, up_own),
            (down_master, down_first, down_second, down_own),
        )
    ]
    gains_done = adam_update(
        norm_gains, factor * gain_total, gains_first, gains_second, gain_rate, 0.0
    )
    return (
        result[None],
        input_grad[None],
        *(part for new in updated for part in new),
        *gains_done,
        grad_norm,
    )


def solution(mesh):
    plan = Plan(mesh)
    by_token = P(("dp", "fsdp"), "ctx", None)
    by_row = P(("dp", "ctx", "fsdp"), None)
    in_specs = (by_token, P(("dp", "fsdp"), "ctx"), by_token) + (by_row,) * 21 + (P(),) * 3
    out_specs = (by_token, by_token) + (by_row,) * 21 + (P(),) * 4
    return jax.shard_map(
        partial(body, plan), mesh=mesh, in_specs=in_specs, out_specs=out_specs, check_vma=False
    )
```

```python
from functools import partial

import jax
import jax.numpy as jnp
from jax import lax
from jax.experimental import pallas as pl
from jax.experimental.pallas import tpu as pltpu
from jax.sharding import PartitionSpec as P

D = 2048
H = 32
HD = 64
KVH = 8
FF = 8192
STEP = 10


eps_norm = 1e-05
rope_base = 1000000.0
clip_bound = 1.0
beta_one = 0.9
beta_two = 0.95
adam_eps = 1e-08
weight_decay = 0.1
weight_rate = 0.04
gain_rate = 0.4
masked = -1e30

BF = jnp.bfloat16
F32 = jnp.float32
GROUP = KVH
QW = H * HD // GROUP
KW = HD
FW = FF // GROUP


class Plan:
    def __init__(self, mesh):
        shape = dict(mesh.shape)
        self.shape = shape
        if shape["dp"] * shape["fsdp"] == GROUP:
            self.tp = ("dp", "fsdp")
        elif shape["dp"] == GROUP:
            self.tp = ("dp",)
        elif shape["fsdp"] == GROUP:
            self.tp = ("fsdp",)
        else:
            raise ValueError("unsupported mesh")
        self.rest = tuple(a for a in ("ctx", "dp", "fsdp") if a not in self.tp)
        self.all = ("dp", "ctx", "fsdp")
        self.two_by_four = self.tp == ("dp", "fsdp") and shape["dp"] == 2

    def me(self):
        return lax.axis_index(self.tp)

    def swap(self, value, bits):
        return lax.ppermute(value, self.tp, [(i, i ^ bits) for i in range(GROUP)])

    def to_inner(self, value):
        lead = value.shape[:-1]
        sizes = [self.shape[a] for a in self.all]
        n = len(lead)
        shaped = value.reshape(*lead, *sizes, -1)
        order = [n + self.all.index(a) for a in self.rest + self.tp]
        return shaped.transpose(*range(n), *order, n + 3).reshape(value.shape)

    def to_outer(self, value):
        lead = value.shape[:-1]
        names = self.rest + self.tp
        sizes = [self.shape[a] for a in names]
        n = len(lead)
        shaped = value.reshape(*lead, *sizes, -1)
        order = [n + names.index(a) for a in self.all]
        return shaped.transpose(*range(n), *order, n + 3).reshape(value.shape)

    def gather_one(self, own):
        if not self.two_by_four:
            return [own] + [self.swap(own, r) for r in range(1, GROUP)]
        return [own, self.swap(own, 2), self.swap(own, 4)]

    def gather_two(self, held):
        if not self.two_by_four:
            return held
        own, by_y, by_x = held
        half = own.shape[0] // 2
        corner = [self.swap(by_y[:half], 4), self.swap(by_x[half:], 2)]
        return [own, self.swap(own, 1), by_y, self.swap(by_y, 1), by_x, *corner]

    def gather_three(self, held):
        if not self.two_by_four:
            return held
        by_x, *corner = held[4:]
        return held[:5] + [self.swap(by_x, 1)] + corner + [self.swap(part, 1) for part in corner]

    def scatter_one(self, blocks):
        if not self.two_by_four:
            return [blocks[0]] + [self.swap(blocks[r], r) for r in range(1, GROUP)]
        return [(blocks[r], self.swap(blocks[r + 1], 1)) for r in range(0, len(blocks), 2)]

    def scatter_two(self, held):
        if not self.two_by_four:
            return held
        left, right = held[3]
        corner = (left.astype(F32) + right.astype(F32)).astype(BF)
        half = corner.shape[0] // 2
        return [*held[:3], self.swap(corner[:half], 4), self.swap(corner[half:], 2)]

    def scatter_three(self, held):
        if not self.two_by_four:
            return held
        own, by_y, by_x, top, low = held
        half = top.shape[0]
        by_y, by_x = [left.astype(F32) + right.astype(F32) for left, right in (by_y, by_x)]
        by_y = jnp.concatenate([by_y[:half] + top.astype(F32), by_y[half:]], axis=0).astype(BF)
        by_x = jnp.concatenate([by_x[:half], by_x[half:] + low.astype(F32)], axis=0).astype(BF)
        return [*own, self.swap(by_y, 2), self.swap(by_x, 4)]

    def scatter_end(self, held):
        total = held[0].astype(F32)
        for part in held[1:]:
            total = total + part.astype(F32)
        return total

    def weight_block(self, stacked):
        got = lax.all_to_all(stacked, self.tp, split_axis=0, concat_axis=0, tiled=True)
        return got.reshape(-1, got.shape[-1])

    def weight_rows(self, block):
        return lax.all_gather(block, self.rest, axis=0, tiled=True)

    def grad_sum(self, grad):
        mine = lax.psum_scatter(grad, self.rest, scatter_dimension=0, tiled=True)
        return mine.reshape(GROUP, -1, grad.shape[1])

    def grad_rows(self, mines, cuts):
        stacked = jnp.concatenate(mines, axis=2)
        got = lax.all_to_all(stacked, self.tp, split_axis=0, concat_axis=0, tiled=True)
        return spread(got, cuts)

    def total(self, value, beside):
        size = 1
        for axis in self.all:
            size *= self.shape[axis]

        def other(bits):
            return lax.ppermute(value, self.all, [(i, i ^ bits) for i in range(size)])

        step = 1
        while step < size:
            if 2 * step < size:
                value = (value + other(step)) + (other(2 * step) + other(3 * step))
            else:
                value = value + other(step)
            if step == 1:
                value, beside = together(value, beside)
            step *= 4
        return value, beside


def rms_scale(values, gain):
    return values * lax.rsqrt(jnp.mean(values * values, axis=-1, keepdims=True) + eps_norm) * gain


def rope_tables(positions):
    half = HD // 2
    freq = rope_base ** (-(jnp.arange(half, dtype=jnp.float32) * 2.0 / HD))
    angle = positions.astype(jnp.float32)[:, None] * freq[None, :]
    cosine, sine = jnp.cos(angle), jnp.sin(angle)
    return (
        jnp.concatenate([cosine] * 4, axis=1),
        jnp.concatenate([-sine, sine, -sine, sine], axis=1),
    )


def across(left, right):
    return lax.dot_general(
        left, right, (((0,), (0,)), ((), ())), preferred_element_type=jnp.float32
    )


def against(left, right):
    return lax.dot_general(
        left, right, (((1,), (1,)), ((), ())), preferred_element_type=jnp.float32
    )


def plain(left, right):
    return jnp.dot(left, right, preferred_element_type=jnp.float32)


def adam_update(weight, grad, first, second, rate, decay):
    first_new = beta_one * first + (1.0 - beta_one) * grad
    second_new = beta_two * second + (1.0 - beta_two) * grad * grad
    ratio = (
        first_new
        / (1.0 - beta_one**STEP)
        / (jnp.sqrt(second_new / (1.0 - beta_two**STEP)) + adam_eps)
    )
    return (first_new, second_new, weight - rate * (ratio + decay * weight))


LANES = 2 * HD


def cost(time):
    return pl.CostEstimate(flops=int(time * 1e9), bytes_accessed=1, transcendentals=0)


def swap_halves(values):
    width = values.shape[-1]
    lane = lax.broadcasted_iota(jnp.int32, values.shape, 1)
    ahead = pltpu.roll(values, width - HD // 2, 1)
    behind = pltpu.roll(values, HD // 2, 1)
    return jnp.where(lane % HD < HD // 2, ahead, behind)


def by_head(values):
    width = values.shape[1]
    row = lax.broadcasted_iota(jnp.int32, (width, width), 0)
    col = lax.broadcasted_iota(jnp.int32, (width, width), 1)
    same = jnp.where(row // HD == col // HD, 1.0 / HD, 0.0).astype(BF)
    high = values.astype(BF)
    low = (values - high.astype(F32)).astype(BF)
    return jnp.dot(high, same, preferred_element_type=F32) + jnp.dot(
        low, same, preferred_element_type=F32
    )


def prepare_kernel(raw_ref, cos_ref, sin_ref, gain_ref, query_ref, kv_ref):
    raw = raw_ref[...]
    heads = raw.shape[1] // HD
    cosine = jnp.concatenate([cos_ref[...]] * (heads // 2), axis=1)
    sine = jnp.concatenate([sin_ref[...]] * (heads // 2), axis=1)
    normed = raw * lax.rsqrt(by_head(raw * raw) + eps_norm) * gain_ref[...]
    turned = normed * cosine + swap_halves(normed) * sine
    query_ref[...] = turned[:, :QW].astype(BF)
    tail = turned[:, QW:]
    lane = lax.broadcasted_iota(jnp.int32, tail.shape, 1)
    kv_ref[...] = jnp.where(lane < KW, tail, raw[:, QW:]).astype(BF)


def prepare(raw, cosine, sine, gains, tile):
    total, width = raw.shape
    return pl.pallas_call(
        prepare_kernel,
        grid=(total // tile,),
        in_specs=[
            pl.BlockSpec((tile, width), lambda i: (i, 0)),
            pl.BlockSpec((tile, LANES), lambda i: (i, 0)),
            pl.BlockSpec((tile, LANES), lambda i: (i, 0)),
            pl.BlockSpec((1, width), lambda i: (0, 0)),
        ],
        out_specs=[
            pl.BlockSpec((tile, QW), lambda i: (i, 0)),
            pl.BlockSpec((tile, LANES), lambda i: (i, 0)),
        ],
        out_shape=[
            jax.ShapeDtypeStruct((total, QW), BF),
            jax.ShapeDtypeStruct((total, LANES), BF),
        ],
        compiler_params=pltpu.CompilerParams(vmem_limit_bytes=24 << 20),
        cost_estimate=cost(6),
    )(raw, cosine, sine, gains)


def unprepare_kernel(n_ctx, raw_ref, cos_ref, sin_ref, gain_ref, dq_ref, *refs):
    parts, (out_ref, dgain_ref) = refs[:n_ctx], refs[n_ctx:]
    raw = raw_ref[...]
    heads = raw.shape[1] // HD
    cosine = jnp.concatenate([cos_ref[...]] * (heads // 2), axis=1)
    sine = jnp.concatenate([sin_ref[...]] * (heads // 2), axis=1)
    gain = gain_ref[...]
    dkv = parts[0][...]
    for part in parts[1:]:
        dkv = dkv + part[...].astype(F32)
    upper = jnp.concatenate([dq_ref[...], dkv], axis=1)
    dnormed = upper * cosine + swap_halves(upper * sine)
    scale = lax.rsqrt(by_head(raw * raw) + eps_norm)
    dgain = dnormed * raw * scale
    inner = dnormed * gain
    draw = scale * inner - raw * (scale * scale * scale) * by_head(inner * raw)
    lane = lax.broadcasted_iota(jnp.int32, upper.shape, 1)
    out_ref[...] = jnp.where(lane < QW + KW, draw, upper).astype(BF)
    total = jnp.sum(dgain, axis=0, keepdims=True)

    @pl.when(pl.program_id(0) == 0)
    def _():
        dgain_ref[...] = total

    @pl.when(pl.program_id(0) > 0)
    def _():
        dgain_ref[...] += total


def unprepare(raw, cosine, sine, gains, dquery, dkv, tile):
    total, width = raw.shape
    kv_spec = pl.BlockSpec((tile, LANES), lambda i: (i, 0))
    return pl.pallas_call(
        partial(unprepare_kernel, len(dkv)),
        grid=(total // tile,),
        in_specs=[
            pl.BlockSpec((tile, width), lambda i: (i, 0)),
            kv_spec,
            kv_spec,
            pl.BlockSpec((1, width), lambda i: (0, 0)),
            pl.BlockSpec((tile, QW), lambda i: (i, 0)),
        ]
        + [kv_spec] * len(dkv),
        out_specs=[
            pl.BlockSpec((tile, width), lambda i: (i, 0)),
            pl.BlockSpec((1, width), lambda i: (0, 0)),
        ],
        out_shape=[
            jax.ShapeDtypeStruct((total, width), BF),
            jax.ShapeDtypeStruct((1, width), F32),
        ],
        compiler_params=pltpu.CompilerParams(vmem_limit_bytes=24 << 20),
        cost_estimate=cost(11),
    )(raw, cosine, sine, gains, dquery, *dkv)


def allowed_bias(base, start, n_ctx, length):
    shape = (n_ctx * length, length)
    key = lax.broadcasted_iota(jnp.int32, shape, 0)
    key_place = base + key % length - (key // length) * length
    place = base + lax.broadcasted_iota(jnp.int32, shape, 1)
    return jnp.where((key_place >= start) & (key_place <= place), 0.0, masked)


def by_rows(left, right):
    return lax.dot_general(
        left, right, (((1,), (1,)), ((), ())), preferred_element_type=jnp.float32
    )


def flash_forward_kernel(n_ctx, base_ref, start_ref, query_ref, *refs):
    kv_refs, (out_ref, log_ref) = refs[:n_ctx], refs[n_ctx:]
    length = query_ref.shape[0]
    kv = jnp.concatenate([ref[...] for ref in kv_refs], axis=0)
    keys, values = kv[:, :HD], kv[:, HD:]
    values_t = values.T
    bias = allowed_bias(base_ref[0], start_ref[0], n_ctx, length)
    outs, logs = [], []
    for head in range(QW // HD):
        query = query_ref[:, head * HD : (head + 1) * HD] * BF(HD**-0.5)
        scores = by_rows(keys, query) + bias
        top = jnp.max(scores, axis=0, keepdims=True)
        weights = jnp.exp(scores - top)
        total = jnp.sum(weights, axis=0, keepdims=True)
        probs = (weights * (1.0 / total)).astype(BF)
        outs.append(jnp.dot(values_t, probs, preferred_element_type=F32))
        logs.append(top + jnp.log(total))
    out_ref[...] = jnp.concatenate(outs, axis=0).T.astype(BF)
    log_ref[0] = jnp.concatenate(logs, axis=0)


def flash_forward(base, starts, query, kv, length):
    total = query.shape[0]
    blocks = total // length
    heads = QW // HD
    n_ctx = len(kv)
    return pl.pallas_call(
        partial(flash_forward_kernel, n_ctx),
        grid=(blocks,),
        in_specs=[
            pl.BlockSpec(memory_space=pltpu.SMEM),
            pl.BlockSpec((1, 1, length), lambda i: (i, 0, 0)),
            pl.BlockSpec((length, QW), lambda i: (i, 0)),
        ]
        + [pl.BlockSpec((length, LANES), lambda i: (i, 0))] * n_ctx,
        out_specs=[
            pl.BlockSpec((length, QW), lambda i: (i, 0)),
            pl.BlockSpec((1, heads, length), lambda i: (i, 0, 0)),
        ],
        out_shape=[
            jax.ShapeDtypeStruct((total, QW), BF),
            jax.ShapeDtypeStruct((blocks, heads, length), F32),
        ],
        compiler_params=pltpu.CompilerParams(vmem_limit_bytes=40 << 20),
        cost_estimate=cost(28),
    )(base, starts, query, *kv)


def flash_backward_kernel(n_ctx, base_ref, start_ref, log_ref, query_ref, upper_ref, *refs):
    kv_refs, dq_ref, dkv_refs = refs[:n_ctx], refs[n_ctx], refs[n_ctx + 1 :]
    length = query_ref.shape[0]
    kv = jnp.concatenate([ref[...] for ref in kv_refs], axis=0)
    keys, values = kv[:, :HD], kv[:, HD:]
    keys_t = keys.T
    bias = allowed_bias(base_ref[0], start_ref[0], n_ctx, length)
    dqs = []
    dkeys = dvalues = None
    for head in range(QW // HD):
        cols = slice(head * HD, (head + 1) * HD)
        query = query_ref[:, cols] * BF(HD**-0.5)
        upper = upper_ref[:, cols]
        scores = by_rows(keys, query) + bias
        probs = jnp.exp(scores - log_ref[0, head : head + 1, :])
        dprobs = by_rows(values, upper)
        delta = jnp.sum(probs * dprobs, axis=0, keepdims=True)
        dscores = (probs * (dprobs - delta)).astype(BF)
        dqs.append(jnp.dot(keys_t, dscores, preferred_element_type=F32) * HD**-0.5)
        dkey = jnp.dot(dscores, query, preferred_element_type=F32)
        dvalue = jnp.dot(probs.astype(BF), upper, preferred_element_type=F32)
        dkeys = dkey if dkeys is None else dkeys + dkey
        dvalues = dvalue if dvalues is None else dvalues + dvalue
    dq_ref[...] = jnp.concatenate(dqs, axis=0).T
    dkv = jnp.concatenate([dkeys, dvalues], axis=1)
    for s in range(n_ctx):
        dkv_refs[s][...] = dkv[s * length : (s + 1) * length].astype(dkv_refs[s].dtype)


def flash_backward(base, starts, logs, query, upper, kv, length):
    total = query.shape[0]
    blocks = total // length
    heads = QW // HD
    n_ctx = len(kv)
    kv_spec = pl.BlockSpec((length, LANES), lambda i: (i, 0))
    q_spec = pl.BlockSpec((length, QW), lambda i: (i, 0))
    return pl.pallas_call(
        partial(flash_backward_kernel, n_ctx),
        grid=(blocks,),
        in_specs=[
            pl.BlockSpec(memory_space=pltpu.SMEM),
            pl.BlockSpec((1, 1, length), lambda i: (i, 0, 0)),
            pl.BlockSpec((1, heads, length), lambda i: (i, 0, 0)),
            q_spec,
            q_spec,
        ]
        + [kv_spec] * n_ctx,
        out_specs=[q_spec] + [kv_spec] * n_ctx,
        out_shape=[jax.ShapeDtypeStruct((total, QW), F32)]
        + [jax.ShapeDtypeStruct((total, LANES), BF if s else F32) for s in range(n_ctx)],
        compiler_params=pltpu.CompilerParams(vmem_limit_bytes=48 << 20),
        cost_estimate=cost(35),
    )(base, starts, logs, query, upper, *kv)


def stack_kernel(*refs):
    parts, out_ref = refs[:-1], refs[-1]
    for p in range(GROUP):
        at = 0
        for part in parts:
            width = part.shape[1] // GROUP
            block = part[:, p * width : (p + 1) * width].astype(BF)
            out_ref[p, :, at : at + width] = block
            at += width


def stack(*parts):
    rows = parts[0].shape[0]
    width = sum(part.shape[1] for part in parts) // GROUP
    return pl.pallas_call(
        stack_kernel,
        in_specs=[pl.BlockSpec(memory_space=pltpu.VMEM)] * len(parts),
        out_specs=pl.BlockSpec(memory_space=pltpu.VMEM),
        out_shape=jax.ShapeDtypeStruct((GROUP, rows, width), BF),
        compiler_params=pltpu.CompilerParams(vmem_limit_bytes=24 << 20),
        cost_estimate=cost(3),
    )(*parts)


def spread_kernel(cuts, stack_ref, *outs):
    for p in range(GROUP):
        for out_ref, (first, width) in zip(outs, cuts):
            out_ref[:, p * width : (p + 1) * width] = stack_ref[p, :, first : first + width]


def spread(stacked, cuts):
    rows = stacked.shape[1]
    return pl.pallas_call(
        partial(spread_kernel, cuts),
        in_specs=[pl.BlockSpec(memory_space=pltpu.VMEM)],
        out_specs=[pl.BlockSpec(memory_space=pltpu.VMEM)] * len(cuts),
        out_shape=[
            jax.ShapeDtypeStruct((rows, GROUP * width), stacked.dtype) for _, width in cuts
        ],
        cost_estimate=cost(2),
    )(stacked)


def columns_kernel(epilogue, n_b, cuts, n_x, *refs):
    blocks, refs = refs[:n_b], refs[n_b:]
    weights, refs = refs[: len(cuts)], refs[len(cuts) :]
    extras, refs = refs[:n_x], refs[n_x:]
    outs, (held, sems) = refs[:-2], refs[-2:]
    chunk = held.shape[0] // 4

    @pl.when(pl.program_id(0) == 0)
    def _():
        copies, start = [], 0
        for r, block in enumerate(blocks):
            there = held.at[pl.ds(start, block.shape[0])]
            copies.append(pltpu.make_async_copy(block, there, sems.at[r]))
            start += block.shape[0]
        for copy in copies:
            copy.start()
        for copy in copies:
            copy.wait()

    @pl.loop(0, 4)
    def _(r):
        rows = pl.ds(pl.multiple_of(r * chunk, chunk), chunk)
        left = held[rows, :]
        sums = [
            jnp.dot(left, w[:, cut], preferred_element_type=F32) for w, cut in zip(weights, cuts)
        ]
        for out, value in zip(outs, epilogue(sums, [x[rows, :] for x in extras])):
            out[rows, :] = value.astype(out.dtype)


def weight_spec(weight, tile, rows):
    array, first, width = weight
    if first % tile:
        return pl.BlockSpec((rows, array.shape[1]), lambda j: (0, 0)), slice(first, first + width)
    return pl.BlockSpec((rows, tile), lambda j: (0, first // tile + j)), slice(0, tile)


def columns(blocks, weights, extras, outs, epilogue, tile):
    n_b = len(blocks)
    depth = blocks[0].shape[1]
    total = sum(block.shape[0] for block in blocks)
    wide = weights[0][2]
    by_tile = pl.BlockSpec((total, tile), lambda j: (0, j))
    specs = [weight_spec(w, tile, depth) for w in weights]
    return pl.pallas_call(
        partial(columns_kernel, epilogue, n_b, [cut for _, cut in specs], len(extras)),
        grid=(wide // tile,),
        in_specs=[pl.BlockSpec(memory_space=pl.ANY)] * n_b
        + [spec for spec, _ in specs]
        + [by_tile] * len(extras),
        out_specs=[by_tile] * len(outs) + [pl.BlockSpec((total, depth), lambda j: (0, 0))],
        out_shape=[jax.ShapeDtypeStruct((total, wide), kind) for kind in outs]
        + [jax.ShapeDtypeStruct((total, depth), BF)],
        scratch_shapes=[pltpu.SemaphoreType.DMA((n_b,))],
        compiler_params=pltpu.CompilerParams(vmem_limit_bytes=52 << 20),
        cost_estimate=cost(2 * total * depth * wide * len(weights) / 6e8 + 3),
    )(*blocks, *[w[0] for w in weights], *extras)


def summed_kernel(left_ref, right_ref, out_ref):
    out_ref[...] = across(left_ref[...], right_ref[...]).astype(BF)


def summed(left, right, tile=512):
    total, depth = left.shape
    wide = right.shape[1]
    return pl.pallas_call(
        summed_kernel,
        grid=(depth // tile,),
        in_specs=[
            pl.BlockSpec((total, tile), lambda j: (0, j)),
            pl.BlockSpec((total, wide), lambda j: (0, 0)),
        ],
        out_specs=pl.BlockSpec((tile, wide), lambda j: (j, 0)),
        out_shape=jax.ShapeDtypeStruct((depth, wide), BF),
        compiler_params=pltpu.CompilerParams(vmem_limit_bytes=44 << 20),
        cost_estimate=cost(2 * total * depth * wide / 6e8 + 1),
    )(left, right)


def back_kernel(n, cuts, picks, *refs):
    lefts, weights, outs = refs[:n], refs[n : 2 * n], refs[2 * n :]
    length = outs[0].shape[0]
    for r, out in zip(picks, outs):
        rows = slice(r * length, (r + 1) * length)
        total = by_rows(lefts[0][rows, :], weights[0][:, cuts[0]])
        for left, weight, cut in zip(lefts[1:], weights[1:], cuts[1:]):
            total = total + by_rows(left[rows, :], weight[:, cut])
        out[...] = total.astype(BF)


def back(lefts, weights, tile, picks=tuple(range(GROUP))):
    total, wide = lefts[0].shape
    depth = weights[0][0].shape[0]
    length = total // GROUP
    n = len(lefts)
    specs, cuts = [], []
    for array, first, width in weights:
        if first % width:
            specs.append(pl.BlockSpec((tile, array.shape[1]), lambda j: (j, 0)))
            cuts.append(slice(first, first + width))
        else:
            specs.append(pl.BlockSpec((tile, width), lambda j, at=first // width: (j, at)))
            cuts.append(slice(0, width))
    return pl.pallas_call(
        partial(back_kernel, n, cuts, picks),
        grid=(depth // tile,),
        in_specs=[pl.BlockSpec((total, wide), lambda j: (0, 0))] * n + specs,
        out_specs=[pl.BlockSpec((length, tile), lambda j: (0, j))] * len(picks),
        out_shape=[jax.ShapeDtypeStruct((length, depth), BF)] * len(picks),
        compiler_params=pltpu.CompilerParams(vmem_limit_bytes=44 << 20),
        cost_estimate=cost(2 * length * len(picks) * depth * wide * n / 6e8 + 1),
    )(*lefts, *[w[0] for w in weights])


def gated(sums, extras):
    gate, upward = sums
    grad = extras[0].astype(F32)
    inverse = 1.0 / (1.0 + jnp.exp(-gate))
    swish = gate * inverse
    return (
        swish * upward,
        grad * upward * (inverse + swish * (1.0 - inverse)),
        grad * swish,
    )


def after(value, *others):
    return lax.optimization_barrier((value,) + others)[0]


def together(*values):
    return lax.optimization_barrier(values)


def after_all(values, *others):
    return lax.optimization_barrier(tuple(values) + others)[: len(values)]


def body(
    plan,
    tokens,
    segment_ids,
    cotangent,
    query_master,
    query_first,
    query_second,
    key_master,
    key_first,
    key_second,
    value_master,
    value_first,
    value_second,
    output_master,
    output_first,
    output_second,
    gate_master,
    gate_first,
    gate_second,
    up_master,
    up_first,
    up_second,
    down_master,
    down_first,
    down_second,
    norm_gains,
    gains_first,
    gains_second,
):
    inputs = plan.to_inner(tokens[0]).astype(F32)
    doc_start = segment_ids[0]
    length = inputs.shape[0]
    n_ctx = plan.shape["ctx"]
    ctx = lax.axis_index("ctx")
    rows = query_master.shape[0]
    gain_one = plan.to_inner(norm_gains[:D])
    gain_two = plan.to_inner(norm_gains[D : 2 * D])
    gain_query = norm_gains[2 * D : 2 * D + HD]
    gain_key = norm_gains[2 * D + HD :]

    starts, step = doc_start, 1
    while step < GROUP:
        starts = jnp.concatenate([starts, plan.swap(starts, step)])
        step *= 2
    total_len = starts.shape[0]
    spots = ctx * length + jnp.arange(length, dtype=jnp.int32)
    cosine, sine = rope_tables(jnp.tile(spots, GROUP) - starts)
    base = (ctx * length).astype(jnp.int32).reshape(1)
    starts_g = starts.reshape(GROUP, 1, length)
    head_gains = jnp.concatenate(
        [jnp.tile(gain_query, QW // HD), gain_key, jnp.ones((HD,), F32)]
    ).reshape(1, -1)
    normed_b = rms_scale(inputs, gain_one).astype(BF)
    out_grad_b = plan.to_inner(cotangent[0])
    down_low, wide_low = stack(down_master), stack(gate_master, up_master)

    attn_block = plan.weight_block(
        stack(query_master, key_master, value_master, output_master)
    )
    attn_block, normed_b, down_low, out_grad_b = together(
        attn_block, normed_b, down_low, out_grad_b
    )
    attn_cols = plan.weight_rows(attn_block)
    held = plan.gather_one(normed_b)
    down_block = plan.weight_block(down_low)
    held, down_block, cosine, sine = together(held, down_block, cosine, sine)
    down_all = plan.weight_rows(down_block)
    held = plan.gather_two(held)
    held, wide_low, attn_cols = together(held, wide_low, attn_cols)
    qkv_w = (attn_cols, 0, QW + 2 * KW)
    out_w = (attn_cols, QW + 2 * KW, QW)
    normed_list = plan.gather_three(held)
    wide_block = plan.weight_block(wide_low)
    qkv, normed_all = columns(normed_list, (qkv_w,), (), (F32,), lambda s, x: s, QW + 2 * KW)
    query_in, own_kv = prepare(qkv, cosine, sine, head_gains, length)

    query_in, own_kv, wide_block, out_grad_b = together(query_in, own_kv, wide_block, out_grad_b)
    kv = [own_kv] + [
        lax.ppermute(own_kv, "ctx", [(i, i + s) for i in range(n_ctx - s)])
        for s in range(1, n_ctx)
    ]
    held = plan.gather_one(out_grad_b)
    kv, held, down_all, wide_block = together(kv, held, down_all, wide_block)
    wide_all = plan.weight_rows(wide_block)
    held = plan.gather_two(held)
    attn_b, logs = flash_forward(base, starts_g, query_in, kv, length)
    attn_b, held = together(attn_b, held)
    gate_w, up_w, down_w = (wide_all, 0, FW), (wide_all, FW, FW), (down_all, 0, FW)
    out_grad_list = plan.gather_three(held)
    blocks = back((attn_b,), (out_w,), 512)
    blocks, out_grad_list = together(blocks, out_grad_list)
    held = plan.scatter_one(blocks)
    held = together(*held)
    held = plan.scatter_two(held)
    held, out_grad_list = together(held, out_grad_list)
    held = plan.scatter_three(held)
    hidden_grad, out_grad_all = columns(out_grad_list, (down_w,), (), (BF,), lambda s, x: s, 512)
    held, hidden_grad, out_grad_all = together(held, hidden_grad, out_grad_all)
    middle = inputs + plan.scatter_end(held)

    normed_two_b = rms_scale(middle, gain_two).astype(BF)
    held = together(*plan.gather_one(normed_two_b))
    held = together(*plan.gather_two(list(held)))
    two_list = plan.gather_three(list(held))
    hidden_b, gate_grad_b, up_grad_b, two_all = columns(
        two_list, (gate_w, up_w), (hidden_grad,), (BF,) * 3, gated, 256
    )
    down_part = summed(out_grad_all, hidden_b)
    gate_grad_b, up_grad_b, hidden_b, two_all, down_part = together(
        gate_grad_b, up_grad_b, hidden_b, two_all, down_part
    )
    down_sum = plan.grad_sum(down_part)
    soon = back((gate_grad_b, up_grad_b), (gate_w, up_w), 512, (7, 6, 5, 4))
    soon, gate_grad_b, up_grad_b, hidden_b = together(soon, gate_grad_b, up_grad_b, hidden_b)
    held_b = plan.scatter_one(list(soon)[::-1]) if plan.two_by_four else list(soon)[::-1]
    late = back((gate_grad_b, up_grad_b), (gate_w, up_w), 512, (3, 2, 1, 0))
    held_b, late, hidden_b, gate_grad_b = together(held_b, late, hidden_b, gate_grad_b)
    if plan.two_by_four:
        held = plan.scatter_two(plan.scatter_one(list(late)[::-1]) + list(held_b))
    else:
        held = plan.scatter_one(list(late)[::-1] + list(held_b))
    gate_part = summed(two_all, gate_grad_b)
    held, gate_part, up_grad_b = together(held, gate_part, up_grad_b)
    gate_sum = plan.grad_sum(gate_part)
    held = plan.scatter_three(held)
    up_part = summed(two_all, up_grad_b)
    held, up_part, hidden_b = together(held, up_part, hidden_b)
    normed_two_grad = plan.scatter_end(held)
    _, norm_two_back = jax.vjp(rms_scale, middle, gain_two)
    middle_norm_grad, gain_two_grad = norm_two_back(normed_two_grad)
    middle_grad = out_grad_b.astype(F32) + middle_norm_grad
    middle_grad_b = middle_grad.astype(BF)

    middle_grad_b, hidden_b = together(middle_grad_b, hidden_b)
    held = plan.gather_one(middle_grad_b)
    blocks = back((hidden_b,), (down_w,), 512)
    held, blocks = together(held, blocks)
    held = plan.gather_two(held)
    out_held = plan.scatter_one(blocks)
    held, out_held = together(held, out_held)
    middle_list = plan.gather_three(held)
    attn_grad_b, middle_all = columns(middle_list, (out_w,), (), (BF,), lambda s, x: s, QW)
    output_part = summed(middle_all, attn_b)
    attn_grad_b, output_part, out_held, down_sum, gate_sum = together(
        attn_grad_b, output_part, out_held, down_sum, gate_sum
    )
    up_sum = plan.grad_sum(up_part)
    out_held = plan.scatter_two(out_held)
    dquery, *dkv = flash_backward(base, starts_g, logs, query_in, attn_grad_b, kv, length)
    dkv = [dkv[0]] + [
        lax.ppermute(dkv[s], "ctx", [(i + s, i) for i in range(n_ctx - s)])
        for s in range(1, n_ctx)
    ]
    out_held = plan.scatter_three(after_all(out_held, dquery))
    sums = after_all((gate_sum, down_sum), dquery)
    gate_own, down_own = plan.grad_rows(sums, [(0, FW), (FW, FW)])
    dkv, out_held, gate_own, down_own, output_part, up_sum = together(
        dkv, out_held, gate_own, down_own, output_part, up_sum
    )
    output_sum = plan.grad_sum(output_part)
    qkv_grad_b, gain_heads = unprepare(qkv, cosine, sine, head_gains, dquery, dkv, length)
    gain_heads = gain_heads.reshape(-1, HD)
    gain_query_grad = jnp.sum(gain_heads[: QW // HD], axis=0)
    gain_key_grad = gain_heads[QW // HD]
    blocks = back((qkv_grad_b,), (qkv_w,), 512)
    blocks, qkv_grad_b = together(blocks, qkv_grad_b)
    held = plan.scatter_one(blocks)
    qkv_part = summed(normed_all, qkv_grad_b)
    held, qkv_part, output_sum = together(held, qkv_part, output_sum)
    qkv_sum = plan.grad_sum(qkv_part)
    held = plan.scatter_two(held)
    held = together(*held)
    result = middle + plan.scatter_end(out_held)
    held = plan.scatter_three(list(held))
    squares = F32(0.0)
    for part in after_all((down_sum, gate_sum, up_sum, output_sum), qkv_part):
        wide = part.astype(F32)
        squares = squares + jnp.sum(wide * wide)
    result = plan.to_outer(result.astype(BF))
    held, squares, result, qkv_sum = together(held, squares, result, qkv_sum)
    normed_grad = plan.scatter_end(held)
    _, norm_one_back = jax.vjp(rms_scale, inputs, gain_one)
    input_norm_grad, gain_one_grad = norm_one_back(normed_grad)
    input_grad = middle_grad + input_norm_grad

    gain_one_grad, gain_two_grad = plan.to_outer(gain_one_grad), plan.to_outer(gain_two_grad)
    qkv_sum, squares, gain_one_grad, gain_two_grad = together(
        qkv_sum, squares, gain_one_grad, gain_two_grad
    )
    wide = qkv_sum.astype(F32)
    squares = squares + jnp.sum(wide * wide)
    gain_part = jnp.concatenate(
        [
            gain_one_grad,
            gain_two_grad,
            gain_query_grad,
            gain_key_grad,
            squares[None],
        ]
    )
    at = QW + 2 * KW
    parts = plan.grad_rows(
        (qkv_sum, output_sum, up_sum), [(0, QW), (QW, 2 * KW), (at, QW), (at + QW, FW)]
    )
    gain_total, (parts, input_grad) = plan.total(gain_part, (parts, plan.to_outer(input_grad)))
    square_total = gain_total[-1]
    gain_total = gain_total[:-1]
    query_own, kv_own, output_own, up_own = parts
    kv_own = kv_own.reshape(rows, GROUP, -1)
    key_own, value_own = [kv_own[:, :, at : at + KW].reshape(rows, -1) for at in (0, KW)]
    grad_norm = jnp.sqrt(square_total + jnp.sum(gain_total * gain_total))
    factor = jnp.minimum(1.0, clip_bound / (grad_norm + 1e-06))
    updated = [
        adam_update(
            weight,
            factor * grads.astype(F32),
            first,
            second,
            weight_rate,
            weight_decay,
        )
        for weight, first, second, grads in (
            (query_master, query_first, query_second, query_own),
            (key_master, key_first, key_second, key_own),
            (value_master, value_first, value_second, value_own),
            (output_master, output_first, output_second, output_own),
            (gate_master, gate_first, gate_second, gate_own),
            (up_master, up_first, up_second, up_own),
            (down_master, down_first, down_second, down_own),
        )
    ]
    gains_done = adam_update(
        norm_gains, factor * gain_total, gains_first, gains_second, gain_rate, 0.0
    )
    return (
        result[None],
        input_grad[None],
        *(part for new in updated for part in new),
        *gains_done,
        grad_norm,
    )


def solution(mesh):
    plan = Plan(mesh)
    by_token = P(("dp", "fsdp"), "ctx", None)
    by_row = P(("dp", "ctx", "fsdp"), None)
    in_specs = (by_token, P(("dp", "fsdp"), "ctx"), by_token) + (by_row,) * 21 + (P(),) * 3
    out_specs = (by_token, by_token) + (by_row,) * 21 + (P(),) * 4
    return jax.shard_map(
        partial(body, plan), mesh=mesh, in_specs=in_specs, out_specs=out_specs, check_vma=False
    )
```

```python
from functools import partial

import jax
import jax.numpy as jnp
from jax import lax
from jax.experimental import pallas as pl
from jax.experimental.pallas import tpu as pltpu
from jax.sharding import PartitionSpec as P

D = 2048
H = 32
HD = 64
KVH = 8
FF = 8192
STEP = 10


eps_norm = 1e-05
rope_base = 1000000.0
clip_bound = 1.0
beta_one = 0.9
beta_two = 0.95
adam_eps = 1e-08
weight_decay = 0.1
weight_rate = 0.04
gain_rate = 0.4
masked = -1e30

BF = jnp.bfloat16
F32 = jnp.float32
GROUP = KVH
QW = H * HD // GROUP
KW = HD
FW = FF // GROUP


class Plan:
    def __init__(self, mesh):
        shape = dict(mesh.shape)
        self.shape = shape
        if shape["dp"] * shape["fsdp"] == GROUP:
            self.tp = ("dp", "fsdp")
        elif shape["dp"] == GROUP:
            self.tp = ("dp",)
        elif shape["fsdp"] == GROUP:
            self.tp = ("fsdp",)
        else:
            raise ValueError("unsupported mesh")
        self.rest = tuple(a for a in ("ctx", "dp", "fsdp") if a not in self.tp)
        self.all = ("dp", "ctx", "fsdp")
        self.two_by_four = self.tp == ("dp", "fsdp") and shape["dp"] == 2

    def me(self):
        return lax.axis_index(self.tp)

    def swap(self, value, bits):
        return lax.ppermute(value, self.tp, [(i, i ^ bits) for i in range(GROUP)])

    def to_inner(self, value):
        lead = value.shape[:-1]
        sizes = [self.shape[a] for a in self.all]
        n = len(lead)
        shaped = value.reshape(*lead, *sizes, -1)
        order = [n + self.all.index(a) for a in self.rest + self.tp]
        return shaped.transpose(*range(n), *order, n + 3).reshape(value.shape)

    def to_outer(self, value):
        lead = value.shape[:-1]
        names = self.rest + self.tp
        sizes = [self.shape[a] for a in names]
        n = len(lead)
        shaped = value.reshape(*lead, *sizes, -1)
        order = [n + names.index(a) for a in self.all]
        return shaped.transpose(*range(n), *order, n + 3).reshape(value.shape)

    def gather_one(self, own):
        if not self.two_by_four:
            return [own] + [self.swap(own, r) for r in range(1, GROUP)]
        return [own, self.swap(own, 2), self.swap(own, 4)]

    def gather_two(self, held):
        if not self.two_by_four:
            return held
        own, by_y, by_x = held
        half = own.shape[0] // 2
        corner = [self.swap(by_y[:half], 4), self.swap(by_x[half:], 2)]
        return [own, self.swap(own, 1), by_y, self.swap(by_y, 1), by_x, *corner]

    def gather_three(self, held):
        if not self.two_by_four:
            return held
        by_x, *corner = held[4:]
        return held[:5] + [self.swap(by_x, 1)] + corner + [self.swap(part, 1) for part in corner]

    def scatter_one(self, blocks):
        if not self.two_by_four:
            return [blocks[0]] + [self.swap(blocks[r], r) for r in range(1, GROUP)]
        return [(blocks[r], self.swap(blocks[r + 1], 1)) for r in range(0, len(blocks), 2)]

    def scatter_two(self, held):
        if not self.two_by_four:
            return held
        left, right = held[3]
        corner = (left.astype(F32) + right.astype(F32)).astype(BF)
        half = corner.shape[0] // 2
        return [*held[:3], self.swap(corner[:half], 4), self.swap(corner[half:], 2)]

    def scatter_three(self, held):
        if not self.two_by_four:
            return held
        own, by_y, by_x, top, low = held
        half = top.shape[0]
        by_y, by_x = [left.astype(F32) + right.astype(F32) for left, right in (by_y, by_x)]
        by_y = jnp.concatenate([by_y[:half] + top.astype(F32), by_y[half:]], axis=0).astype(BF)
        by_x = jnp.concatenate([by_x[:half], by_x[half:] + low.astype(F32)], axis=0).astype(BF)
        return [*own, self.swap(by_y, 2), self.swap(by_x, 4)]

    def scatter_end(self, held):
        total = held[0].astype(F32)
        for part in held[1:]:
            total = total + part.astype(F32)
        return total

    def weight_block(self, stacked):
        got = lax.all_to_all(stacked, self.tp, split_axis=0, concat_axis=0, tiled=True)
        return got.reshape(-1, got.shape[-1])

    def weight_rows(self, block):
        return lax.all_gather(block, self.rest, axis=0, tiled=True)

    def grad_sum(self, grad):
        mine = lax.psum_scatter(grad, self.rest, scatter_dimension=0, tiled=True)
        return mine.reshape(GROUP, -1, grad.shape[1])

    def grad_rows(self, mines, cuts):
        stacked = jnp.concatenate(mines, axis=2)
        got = lax.all_to_all(stacked, self.tp, split_axis=0, concat_axis=0, tiled=True)
        return spread(got, cuts)

    def total(self, value, beside):
        size = 1
        for axis in self.all:
            size *= self.shape[axis]

        def other(bits):
            return lax.ppermute(value, self.all, [(i, i ^ bits) for i in range(size)])

        step = 1
        while step < size:
            if 2 * step < size:
                value = (value + other(step)) + (other(2 * step) + other(3 * step))
            else:
                value = value + other(step)
            if step == 1:
                value, beside = together(value, beside)
            step *= 4
        return value, beside


def rms_scale(values, gain):
    return values * lax.rsqrt(jnp.mean(values * values, axis=-1, keepdims=True) + eps_norm) * gain


def rope_tables(positions):
    half = HD // 2
    freq = rope_base ** (-(jnp.arange(half, dtype=jnp.float32) * 2.0 / HD))
    angle = positions.astype(jnp.float32)[:, None] * freq[None, :]
    cosine, sine = jnp.cos(angle), jnp.sin(angle)
    return (
        jnp.concatenate([cosine] * 4, axis=1),
        jnp.concatenate([-sine, sine, -sine, sine], axis=1),
    )


def across(left, right):
    return lax.dot_general(
        left, right, (((0,), (0,)), ((), ())), preferred_element_type=jnp.float32
    )


def against(left, right):
    return lax.dot_general(
        left, right, (((1,), (1,)), ((), ())), preferred_element_type=jnp.float32
    )


def plain(left, right):
    return jnp.dot(left, right, preferred_element_type=jnp.float32)


def adam_update(weight, grad, first, second, rate, decay):
    first_new = beta_one * first + (1.0 - beta_one) * grad
    second_new = beta_two * second + (1.0 - beta_two) * grad * grad
    ratio = (
        first_new
        / (1.0 - beta_one**STEP)
        / (jnp.sqrt(second_new / (1.0 - beta_two**STEP)) + adam_eps)
    )
    return (first_new, second_new, weight - rate * (ratio + decay * weight))


LANES = 2 * HD


def cost(time):
    return pl.CostEstimate(flops=int(time * 1e9), bytes_accessed=1, transcendentals=0)


def swap_halves(values):
    width = values.shape[-1]
    lane = lax.broadcasted_iota(jnp.int32, values.shape, 1)
    ahead = pltpu.roll(values, width - HD // 2, 1)
    behind = pltpu.roll(values, HD // 2, 1)
    return jnp.where(lane % HD < HD // 2, ahead, behind)


def by_head(values):
    width = values.shape[1]
    row = lax.broadcasted_iota(jnp.int32, (width, width), 0)
    col = lax.broadcasted_iota(jnp.int32, (width, width), 1)
    same = jnp.where(row // HD == col // HD, 1.0 / HD, 0.0).astype(BF)
    high = values.astype(BF)
    low = (values - high.astype(F32)).astype(BF)
    return jnp.dot(high, same, preferred_element_type=F32) + jnp.dot(
        low, same, preferred_element_type=F32
    )


def prepare_kernel(raw_ref, cos_ref, sin_ref, gain_ref, query_ref, kv_ref):
    raw = raw_ref[...]
    heads = raw.shape[1] // HD
    cosine = jnp.concatenate([cos_ref[...]] * (heads // 2), axis=1)
    sine = jnp.concatenate([sin_ref[...]] * (heads // 2), axis=1)
    normed = raw * lax.rsqrt(by_head(raw * raw) + eps_norm) * gain_ref[...]
    turned = normed * cosine + swap_halves(normed) * sine
    query_ref[...] = turned[:, :QW].astype(BF)
    tail = turned[:, QW:]
    lane = lax.broadcasted_iota(jnp.int32, tail.shape, 1)
    kv_ref[...] = jnp.where(lane < KW, tail, raw[:, QW:]).astype(BF)


def prepare(raw, cosine, sine, gains, tile):
    total, width = raw.shape
    return pl.pallas_call(
        prepare_kernel,
        grid=(total // tile,),
        in_specs=[
            pl.BlockSpec((tile, width), lambda i: (i, 0)),
            pl.BlockSpec((tile, LANES), lambda i: (i, 0)),
            pl.BlockSpec((tile, LANES), lambda i: (i, 0)),
            pl.BlockSpec((1, width), lambda i: (0, 0)),
        ],
        out_specs=[
            pl.BlockSpec((tile, QW), lambda i: (i, 0)),
            pl.BlockSpec((tile, LANES), lambda i: (i, 0)),
        ],
        out_shape=[
            jax.ShapeDtypeStruct((total, QW), BF),
            jax.ShapeDtypeStruct((total, LANES), BF),
        ],
        compiler_params=pltpu.CompilerParams(vmem_limit_bytes=24 << 20),
        cost_estimate=cost(6),
    )(raw, cosine, sine, gains)


def unprepare_kernel(n_ctx, raw_ref, cos_ref, sin_ref, gain_ref, dq_ref, *refs):
    parts, (out_ref, dgain_ref) = refs[:n_ctx], refs[n_ctx:]
    raw = raw_ref[...]
    heads = raw.shape[1] // HD
    cosine = jnp.concatenate([cos_ref[...]] * (heads // 2), axis=1)
    sine = jnp.concatenate([sin_ref[...]] * (heads // 2), axis=1)
    gain = gain_ref[...]
    dkv = parts[0][...]
    for part in parts[1:]:
        dkv = dkv + part[...].astype(F32)
    upper = jnp.concatenate([dq_ref[...], dkv], axis=1)
    dnormed = upper * cosine + swap_halves(upper * sine)
    scale = lax.rsqrt(by_head(raw * raw) + eps_norm)
    dgain = dnormed * raw * scale
    inner = dnormed * gain
    draw = scale * inner - raw * (scale * scale * scale) * by_head(inner * raw)
    lane = lax.broadcasted_iota(jnp.int32, upper.shape, 1)
    out_ref[...] = jnp.where(lane < QW + KW, draw, upper).astype(BF)
    total = jnp.sum(dgain, axis=0, keepdims=True)

    @pl.when(pl.program_id(0) == 0)
    def _():
        dgain_ref[...] = total

    @pl.when(pl.program_id(0) > 0)
    def _():
        dgain_ref[...] += total


def unprepare(raw, cosine, sine, gains, dquery, dkv, tile):
    total, width = raw.shape
    kv_spec = pl.BlockSpec((tile, LANES), lambda i: (i, 0))
    return pl.pallas_call(
        partial(unprepare_kernel, len(dkv)),
        grid=(total // tile,),
        in_specs=[
            pl.BlockSpec((tile, width), lambda i: (i, 0)),
            kv_spec,
            kv_spec,
            pl.BlockSpec((1, width), lambda i: (0, 0)),
            pl.BlockSpec((tile, QW), lambda i: (i, 0)),
        ]
        + [kv_spec] * len(dkv),
        out_specs=[
            pl.BlockSpec((tile, width), lambda i: (i, 0)),
            pl.BlockSpec((1, width), lambda i: (0, 0)),
        ],
        out_shape=[
            jax.ShapeDtypeStruct((total, width), BF),
            jax.ShapeDtypeStruct((1, width), F32),
        ],
        compiler_params=pltpu.CompilerParams(vmem_limit_bytes=24 << 20),
        cost_estimate=cost(11),
    )(raw, cosine, sine, gains, dquery, *dkv)


def allowed_bias(base, start, n_ctx, length):
    shape = (length, length)
    key = base + lax.broadcasted_iota(jnp.int32, shape, 0)
    place = base + lax.broadcasted_iota(jnp.int32, shape, 1)
    blocks = []
    for s in range(n_ctx):
        key_place = key - s * length
        blocks.append(jnp.where((key_place >= start) & (key_place <= place), 0.0, masked))
    return jnp.concatenate(blocks, axis=0)


def by_rows(left, right):
    return lax.dot_general(
        left, right, (((1,), (1,)), ((), ())), preferred_element_type=jnp.float32
    )


def flash_forward_kernel(n_ctx, base_ref, start_ref, query_ref, *refs):
    kv_refs, (out_ref, log_ref) = refs[:n_ctx], refs[n_ctx:]
    length = query_ref.shape[0]
    kv = jnp.concatenate([ref[...] for ref in kv_refs], axis=0)
    keys, values = kv[:, :HD], kv[:, HD:]
    values_t = values.T
    bias = allowed_bias(base_ref[0], start_ref[0], n_ctx, length)
    outs, logs = [], []
    for head in range(QW // HD):
        query = query_ref[:, head * HD : (head + 1) * HD] * BF(HD**-0.5)
        scores = by_rows(keys, query) + bias
        top = jnp.max(scores, axis=0, keepdims=True)
        weights = jnp.exp(scores - top)
        total = jnp.sum(weights, axis=0, keepdims=True)
        probs = (weights * (1.0 / total)).astype(BF)
        outs.append(jnp.dot(values_t, probs, preferred_element_type=F32))
        logs.append(top + jnp.log(total))
    out_ref[...] = jnp.concatenate(outs, axis=0).T.astype(BF)
    log_ref[0] = jnp.concatenate(logs, axis=0)


def flash_forward(base, starts, query, kv, length):
    total = query.shape[0]
    blocks = total // length
    heads = QW // HD
    n_ctx = len(kv)
    return pl.pallas_call(
        partial(flash_forward_kernel, n_ctx),
        grid=(blocks,),
        in_specs=[
            pl.BlockSpec(memory_space=pltpu.SMEM),
            pl.BlockSpec((1, 1, length), lambda i: (i, 0, 0)),
            pl.BlockSpec((length, QW), lambda i: (i, 0)),
        ]
        + [pl.BlockSpec((length, LANES), lambda i: (i, 0))] * n_ctx,
        out_specs=[
            pl.BlockSpec((length, QW), lambda i: (i, 0)),
            pl.BlockSpec((1, heads, length), lambda i: (i, 0, 0)),
        ],
        out_shape=[
            jax.ShapeDtypeStruct((total, QW), BF),
            jax.ShapeDtypeStruct((blocks, heads, length), F32),
        ],
        compiler_params=pltpu.CompilerParams(vmem_limit_bytes=40 << 20),
        cost_estimate=cost(28),
    )(base, starts, query, *kv)


def flash_backward_kernel(n_ctx, base_ref, start_ref, log_ref, query_ref, upper_ref, *refs):
    kv_refs, dq_ref, dkv_refs = refs[:n_ctx], refs[n_ctx], refs[n_ctx + 1 :]
    length = query_ref.shape[0]
    kv = jnp.concatenate([ref[...] for ref in kv_refs], axis=0)
    keys, values = kv[:, :HD], kv[:, HD:]
    keys_t = keys.T
    bias = allowed_bias(base_ref[0], start_ref[0], n_ctx, length)
    dqs = []
    dkeys = dvalues = None
    for head in range(QW // HD):
        cols = slice(head * HD, (head + 1) * HD)
        query = query_ref[:, cols] * BF(HD**-0.5)
        upper = upper_ref[:, cols]
        scores = by_rows(keys, query) + bias
        probs = jnp.exp(scores - log_ref[0, head : head + 1, :])
        dprobs = by_rows(values, upper)
        delta = jnp.sum(probs * dprobs, axis=0, keepdims=True)
        dscores = (probs * (dprobs - delta)).astype(BF)
        dqs.append(jnp.dot(keys_t, dscores, preferred_element_type=F32) * HD**-0.5)
        dkey = jnp.dot(dscores, query, preferred_element_type=F32)
        dvalue = jnp.dot(probs.astype(BF), upper, preferred_element_type=F32)
        dkeys = dkey if dkeys is None else dkeys + dkey
        dvalues = dvalue if dvalues is None else dvalues + dvalue
    dq_ref[...] = jnp.concatenate(dqs, axis=0).T
    dkv = jnp.concatenate([dkeys, dvalues], axis=1)
    for s in range(n_ctx):
        dkv_refs[s][...] = dkv[s * length : (s + 1) * length].astype(dkv_refs[s].dtype)


def flash_backward(base, starts, logs, query, upper, kv, length):
    total = query.shape[0]
    blocks = total // length
    heads = QW // HD
    n_ctx = len(kv)
    kv_spec = pl.BlockSpec((length, LANES), lambda i: (i, 0))
    q_spec = pl.BlockSpec((length, QW), lambda i: (i, 0))
    return pl.pallas_call(
        partial(flash_backward_kernel, n_ctx),
        grid=(blocks,),
        in_specs=[
            pl.BlockSpec(memory_space=pltpu.SMEM),
            pl.BlockSpec((1, 1, length), lambda i: (i, 0, 0)),
            pl.BlockSpec((1, heads, length), lambda i: (i, 0, 0)),
            q_spec,
            q_spec,
        ]
        + [kv_spec] * n_ctx,
        out_specs=[q_spec] + [kv_spec] * n_ctx,
        out_shape=[jax.ShapeDtypeStruct((total, QW), F32)]
        + [jax.ShapeDtypeStruct((total, LANES), BF if s else F32) for s in range(n_ctx)],
        compiler_params=pltpu.CompilerParams(vmem_limit_bytes=48 << 20),
        cost_estimate=cost(35),
    )(base, starts, logs, query, upper, *kv)


def stack_kernel(*refs):
    parts, out_ref = refs[:-1], refs[-1]
    for p in range(GROUP):
        at = 0
        for part in parts:
            width = part.shape[1] // GROUP
            block = part[:, p * width : (p + 1) * width].astype(BF)
            out_ref[p, :, at : at + width] = block
            at += width


def stack(*parts):
    rows = parts[0].shape[0]
    width = sum(part.shape[1] for part in parts) // GROUP
    return pl.pallas_call(
        stack_kernel,
        in_specs=[pl.BlockSpec(memory_space=pltpu.VMEM)] * len(parts),
        out_specs=pl.BlockSpec(memory_space=pltpu.VMEM),
        out_shape=jax.ShapeDtypeStruct((GROUP, rows, width), BF),
        compiler_params=pltpu.CompilerParams(vmem_limit_bytes=24 << 20),
        cost_estimate=cost(3),
    )(*parts)


def spread_kernel(cuts, stack_ref, *outs):
    for p in range(GROUP):
        for out_ref, (first, width) in zip(outs, cuts):
            out_ref[:, p * width : (p + 1) * width] = stack_ref[p, :, first : first + width]


def spread(stacked, cuts):
    rows = stacked.shape[1]
    return pl.pallas_call(
        partial(spread_kernel, cuts),
        in_specs=[pl.BlockSpec(memory_space=pltpu.VMEM)],
        out_specs=[pl.BlockSpec(memory_space=pltpu.VMEM)] * len(cuts),
        out_shape=[
            jax.ShapeDtypeStruct((rows, GROUP * width), stacked.dtype) for _, width in cuts
        ],
        cost_estimate=cost(2),
    )(stacked)


def columns_kernel(epilogue, n_b, cuts, n_x, *refs):
    blocks, refs = refs[:n_b], refs[n_b:]
    weights, refs = refs[: len(cuts)], refs[len(cuts) :]
    extras, refs = refs[:n_x], refs[n_x:]
    outs, (held, sems) = refs[:-2], refs[-2:]
    chunk = held.shape[0] // 4

    @pl.when(pl.program_id(0) == 0)
    def _():
        copies, start = [], 0
        for r, block in enumerate(blocks):
            there = held.at[pl.ds(start, block.shape[0])]
            copies.append(pltpu.make_async_copy(block, there, sems.at[r]))
            start += block.shape[0]
        for copy in copies:
            copy.start()
        for copy in copies:
            copy.wait()

    @pl.loop(0, 4)
    def _(r):
        rows = pl.ds(pl.multiple_of(r * chunk, chunk), chunk)
        left = held[rows, :]
        sums = [
            jnp.dot(left, w[:, cut], preferred_element_type=F32) for w, cut in zip(weights, cuts)
        ]
        for out, value in zip(outs, epilogue(sums, [x[rows, :] for x in extras])):
            out[rows, :] = value.astype(out.dtype)


def weight_spec(weight, tile, rows):
    array, first, width = weight
    if first % tile:
        return pl.BlockSpec((rows, array.shape[1]), lambda j: (0, 0)), slice(first, first + width)
    return pl.BlockSpec((rows, tile), lambda j: (0, first // tile + j)), slice(0, tile)


def columns(blocks, weights, extras, outs, epilogue, tile):
    n_b = len(blocks)
    depth = blocks[0].shape[1]
    total = sum(block.shape[0] for block in blocks)
    wide = weights[0][2]
    by_tile = pl.BlockSpec((total, tile), lambda j: (0, j))
    specs = [weight_spec(w, tile, depth) for w in weights]
    return pl.pallas_call(
        partial(columns_kernel, epilogue, n_b, [cut for _, cut in specs], len(extras)),
        grid=(wide // tile,),
        in_specs=[pl.BlockSpec(memory_space=pl.ANY)] * n_b
        + [spec for spec, _ in specs]
        + [by_tile] * len(extras),
        out_specs=[by_tile] * len(outs) + [pl.BlockSpec((total, depth), lambda j: (0, 0))],
        out_shape=[jax.ShapeDtypeStruct((total, wide), kind) for kind in outs]
        + [jax.ShapeDtypeStruct((total, depth), BF)],
        scratch_shapes=[pltpu.SemaphoreType.DMA((n_b,))],
        compiler_params=pltpu.CompilerParams(vmem_limit_bytes=52 << 20),
        cost_estimate=cost(2 * total * depth * wide * len(weights) / 6e8 + 3),
    )(*blocks, *[w[0] for w in weights], *extras)


def summed_kernel(left_ref, right_ref, out_ref):
    out_ref[...] = across(left_ref[...], right_ref[...]).astype(BF)


def summed(left, right, tile=512):
    total, depth = left.shape
    wide = right.shape[1]
    return pl.pallas_call(
        summed_kernel,
        grid=(depth // tile,),
        in_specs=[
            pl.BlockSpec((total, tile), lambda j: (0, j)),
            pl.BlockSpec((total, wide), lambda j: (0, 0)),
        ],
        out_specs=pl.BlockSpec((tile, wide), lambda j: (j, 0)),
        out_shape=jax.ShapeDtypeStruct((depth, wide), BF),
        compiler_params=pltpu.CompilerParams(vmem_limit_bytes=44 << 20),
        cost_estimate=cost(2 * total * depth * wide / 6e8 + 1),
    )(left, right)


def back_kernel(n, cuts, picks, *refs):
    lefts, weights, outs = refs[:n], refs[n : 2 * n], refs[2 * n :]
    length = outs[0].shape[0]
    for r, out in zip(picks, outs):
        rows = slice(r * length, (r + 1) * length)
        total = by_rows(lefts[0][rows, :], weights[0][:, cuts[0]])
        for left, weight, cut in zip(lefts[1:], weights[1:], cuts[1:]):
            total = total + by_rows(left[rows, :], weight[:, cut])
        out[...] = total.astype(BF)


def back(lefts, weights, tile, picks=tuple(range(GROUP))):
    total, wide = lefts[0].shape
    depth = weights[0][0].shape[0]
    length = total // GROUP
    n = len(lefts)
    specs, cuts = [], []
    for array, first, width in weights:
        if first % width:
            specs.append(pl.BlockSpec((tile, array.shape[1]), lambda j: (j, 0)))
            cuts.append(slice(first, first + width))
        else:
            specs.append(pl.BlockSpec((tile, width), lambda j, at=first // width: (j, at)))
            cuts.append(slice(0, width))
    return pl.pallas_call(
        partial(back_kernel, n, cuts, picks),
        grid=(depth // tile,),
        in_specs=[pl.BlockSpec((total, wide), lambda j: (0, 0))] * n + specs,
        out_specs=[pl.BlockSpec((length, tile), lambda j: (0, j))] * len(picks),
        out_shape=[jax.ShapeDtypeStruct((length, depth), BF)] * len(picks),
        compiler_params=pltpu.CompilerParams(vmem_limit_bytes=44 << 20),
        cost_estimate=cost(2 * length * len(picks) * depth * wide * n / 6e8 + 1),
    )(*lefts, *[w[0] for w in weights])


def gated(sums, extras):
    gate, upward = sums
    grad = extras[0].astype(F32)
    inverse = 1.0 / (1.0 + jnp.exp(-gate))
    swish = gate * inverse
    return (
        swish * upward,
        grad * upward * (inverse + swish * (1.0 - inverse)),
        grad * swish,
    )


def after(value, *others):
    return lax.optimization_barrier((value,) + others)[0]


def together(*values):
    return lax.optimization_barrier(values)


def after_all(values, *others):
    return lax.optimization_barrier(tuple(values) + others)[: len(values)]


def body(
    plan,
    tokens,
    segment_ids,
    cotangent,
    query_master,
    query_first,
    query_second,
    key_master,
    key_first,
    key_second,
    value_master,
    value_first,
    value_second,
    output_master,
    output_first,
    output_second,
    gate_master,
    gate_first,
    gate_second,
    up_master,
    up_first,
    up_second,
    down_master,
    down_first,
    down_second,
    norm_gains,
    gains_first,
    gains_second,
):
    inputs = plan.to_inner(tokens[0]).astype(F32)
    doc_start = segment_ids[0]
    length = inputs.shape[0]
    n_ctx = plan.shape["ctx"]
    ctx = lax.axis_index("ctx")
    rows = query_master.shape[0]
    gain_one = plan.to_inner(norm_gains[:D])
    gain_two = plan.to_inner(norm_gains[D : 2 * D])
    gain_query = norm_gains[2 * D : 2 * D + HD]
    gain_key = norm_gains[2 * D + HD :]

    starts, step = doc_start, 1
    while step < GROUP:
        starts = jnp.concatenate([starts, plan.swap(starts, step)])
        step *= 2
    total_len = starts.shape[0]
    spots = ctx * length + jnp.arange(length, dtype=jnp.int32)
    cosine, sine = rope_tables(jnp.tile(spots, GROUP) - starts)
    base = (ctx * length).astype(jnp.int32).reshape(1)
    starts_g = starts.reshape(GROUP, 1, length)
    head_gains = jnp.concatenate(
        [jnp.tile(gain_query, QW // HD), gain_key, jnp.ones((HD,), F32)]
    ).reshape(1, -1)
    normed_b = rms_scale(inputs, gain_one).astype(BF)
    out_grad_b = plan.to_inner(cotangent[0])
    down_low, wide_low = stack(down_master), stack(gate_master, up_master)

    attn_block = plan.weight_block(
        stack(query_master, key_master, value_master, output_master)
    )
    attn_block, normed_b, down_low, out_grad_b = together(
        attn_block, normed_b, down_low, out_grad_b
    )
    attn_cols = plan.weight_rows(attn_block)
    held = plan.gather_one(normed_b)
    down_block = plan.weight_block(down_low)
    held, down_block, cosine, sine = together(held, down_block, cosine, sine)
    down_all = plan.weight_rows(down_block)
    held = plan.gather_two(held)
    held, wide_low, attn_cols = together(held, wide_low, attn_cols)
    qkv_w = (attn_cols, 0, QW + 2 * KW)
    out_w = (attn_cols, QW + 2 * KW, QW)
    normed_list = plan.gather_three(held)
    wide_block = plan.weight_block(wide_low)
    qkv, normed_all = columns(normed_list, (qkv_w,), (), (F32,), lambda s, x: s, QW + 2 * KW)
    query_in, own_kv = prepare(qkv, cosine, sine, head_gains, length)

    query_in, own_kv, wide_block, out_grad_b = together(query_in, own_kv, wide_block, out_grad_b)
    kv = [own_kv] + [
        lax.ppermute(own_kv, "ctx", [(i, i + s) for i in range(n_ctx - s)])
        for s in range(1, n_ctx)
    ]
    held = plan.gather_one(out_grad_b)
    kv, held, down_all, wide_block = together(kv, held, down_all, wide_block)
    wide_all = plan.weight_rows(wide_block)
    held = plan.gather_two(held)
    attn_b, logs = flash_forward(base, starts_g, query_in, kv, length)
    attn_b, held = together(attn_b, held)
    gate_w, up_w, down_w = (wide_all, 0, FW), (wide_all, FW, FW), (down_all, 0, FW)
    out_grad_list = plan.gather_three(held)
    blocks = back((attn_b,), (out_w,), 512)
    blocks, out_grad_list = together(blocks, out_grad_list)
    held = plan.scatter_one(blocks)
    held = together(*held)
    held = plan.scatter_two(held)
    held, out_grad_list = together(held, out_grad_list)
    held = plan.scatter_three(held)
    hidden_grad, out_grad_all = columns(out_grad_list, (down_w,), (), (BF,), lambda s, x: s, 512)
    held, hidden_grad, out_grad_all = together(held, hidden_grad, out_grad_all)
    middle = inputs + plan.scatter_end(held)

    normed_two_b = rms_scale(middle, gain_two).astype(BF)
    held = together(*plan.gather_one(normed_two_b))
    held = together(*plan.gather_two(list(held)))
    two_list = plan.gather_three(list(held))
    hidden_b, gate_grad_b, up_grad_b, two_all = columns(
        two_list, (gate_w, up_w), (hidden_grad,), (BF,) * 3, gated, 256
    )
    down_part = summed(out_grad_all, hidden_b)
    gate_grad_b, up_grad_b, hidden_b, two_all, down_part = together(
        gate_grad_b, up_grad_b, hidden_b, two_all, down_part
    )
    down_sum = plan.grad_sum(down_part)
    soon = back((gate_grad_b, up_grad_b), (gate_w, up_w), 512, (7, 6, 5, 4))
    soon, gate_grad_b, up_grad_b, hidden_b = together(soon, gate_grad_b, up_grad_b, hidden_b)
    held_b = plan.scatter_one(list(soon)[::-1]) if plan.two_by_four else list(soon)[::-1]
    late = back((gate_grad_b, up_grad_b), (gate_w, up_w), 512, (3, 2, 1, 0))
    held_b, late, hidden_b, gate_grad_b = together(held_b, late, hidden_b, gate_grad_b)
    if plan.two_by_four:
        held = plan.scatter_two(plan.scatter_one(list(late)[::-1]) + list(held_b))
    else:
        held = plan.scatter_one(list(late)[::-1] + list(held_b))
    gate_part = summed(two_all, gate_grad_b)
    held, gate_part, up_grad_b = together(held, gate_part, up_grad_b)
    gate_sum = plan.grad_sum(gate_part)
    held = plan.scatter_three(held)
    up_part = summed(two_all, up_grad_b)
    held, up_part, hidden_b = together(held, up_part, hidden_b)
    normed_two_grad = plan.scatter_end(held)
    _, norm_two_back = jax.vjp(rms_scale, middle, gain_two)
    middle_norm_grad, gain_two_grad = norm_two_back(normed_two_grad)
    middle_grad = out_grad_b.astype(F32) + middle_norm_grad
    middle_grad_b = middle_grad.astype(BF)

    middle_grad_b, hidden_b = together(middle_grad_b, hidden_b)
    held = plan.gather_one(middle_grad_b)
    blocks = back((hidden_b,), (down_w,), 512)
    held, blocks = together(held, blocks)
    held = plan.gather_two(held)
    out_held = plan.scatter_one(blocks)
    held, out_held = together(held, out_held)
    middle_list = plan.gather_three(held)
    attn_grad_b, middle_all = columns(middle_list, (out_w,), (), (BF,), lambda s, x: s, QW)
    output_part = summed(middle_all, attn_b)
    attn_grad_b, output_part, out_held, down_sum, gate_sum = together(
        attn_grad_b, output_part, out_held, down_sum, gate_sum
    )
    up_sum = plan.grad_sum(up_part)
    out_held = plan.scatter_two(out_held)
    dquery, *dkv = flash_backward(base, starts_g, logs, query_in, attn_grad_b, kv, length)
    dkv = [dkv[0]] + [
        lax.ppermute(dkv[s], "ctx", [(i + s, i) for i in range(n_ctx - s)])
        for s in range(1, n_ctx)
    ]
    out_held = plan.scatter_three(after_all(out_held, dquery))
    sums = after_all((gate_sum, down_sum), dquery)
    gate_own, down_own = plan.grad_rows(sums, [(0, FW), (FW, FW)])
    dkv, out_held, gate_own, down_own, output_part, up_sum = together(
        dkv, out_held, gate_own, down_own, output_part, up_sum
    )
    output_sum = plan.grad_sum(output_part)
    qkv_grad_b, gain_heads = unprepare(qkv, cosine, sine, head_gains, dquery, dkv, length)
    gain_heads = gain_heads.reshape(-1, HD)
    gain_query_grad = jnp.sum(gain_heads[: QW // HD], axis=0)
    gain_key_grad = gain_heads[QW // HD]
    blocks = back((qkv_grad_b,), (qkv_w,), 512)
    blocks, qkv_grad_b = together(blocks, qkv_grad_b)
    held = plan.scatter_one(blocks)
    qkv_part = summed(normed_all, qkv_grad_b)
    held, qkv_part, output_sum = together(held, qkv_part, output_sum)
    qkv_sum = plan.grad_sum(qkv_part)
    held = plan.scatter_two(held)
    held = together(*held)
    result = middle + plan.scatter_end(out_held)
    held = plan.scatter_three(list(held))
    squares = F32(0.0)
    for part in after_all((down_sum, gate_sum, up_sum, output_sum), qkv_part):
        wide = part.astype(F32)
        squares = squares + jnp.sum(wide * wide)
    result = plan.to_outer(result.astype(BF))
    held, squares, result, qkv_sum = together(held, squares, result, qkv_sum)
    normed_grad = plan.scatter_end(held)
    _, norm_one_back = jax.vjp(rms_scale, inputs, gain_one)
    input_norm_grad, gain_one_grad = norm_one_back(normed_grad)
    input_grad = middle_grad + input_norm_grad

    gain_one_grad, gain_two_grad = plan.to_outer(gain_one_grad), plan.to_outer(gain_two_grad)
    qkv_sum, squares, gain_one_grad, gain_two_grad = together(
        qkv_sum, squares, gain_one_grad, gain_two_grad
    )
    wide = qkv_sum.astype(F32)
    squares = squares + jnp.sum(wide * wide)
    gain_part = jnp.concatenate(
        [
            gain_one_grad,
            gain_two_grad,
            gain_query_grad,
            gain_key_grad,
            squares[None],
        ]
    )
    at = QW + 2 * KW
    parts = plan.grad_rows(
        (qkv_sum, output_sum, up_sum), [(0, QW), (QW, 2 * KW), (at, QW), (at + QW, FW)]
    )
    gain_total, (parts, input_grad) = plan.total(gain_part, (parts, plan.to_outer(input_grad)))
    square_total = gain_total[-1]
    gain_total = gain_total[:-1]
    query_own, kv_own, output_own, up_own = parts
    kv_own = kv_own.reshape(rows, GROUP, -1)
    key_own, value_own = [kv_own[:, :, at : at + KW].reshape(rows, -1) for at in (0, KW)]
    grad_norm = jnp.sqrt(square_total + jnp.sum(gain_total * gain_total))
    factor = jnp.minimum(1.0, clip_bound / (grad_norm + 1e-06))
    updated = [
        adam_update(
            weight,
            factor * grads.astype(F32),
            first,
            second,
            weight_rate,
            weight_decay,
        )
        for weight, first, second, grads in (
            (query_master, query_first, query_second, query_own),
            (key_master, key_first, key_second, key_own),
            (value_master, value_first, value_second, value_own),
            (output_master, output_first, output_second, output_own),
            (gate_master, gate_first, gate_second, gate_own),
            (up_master, up_first, up_second, up_own),
            (down_master, down_first, down_second, down_own),
        )
    ]
    gains_done = adam_update(
        norm_gains, factor * gain_total, gains_first, gains_second, gain_rate, 0.0
    )
    return (
        result[None],
        input_grad[None],
        *(part for new in updated for part in new),
        *gains_done,
        grad_norm,
    )


def solution(mesh):
    plan = Plan(mesh)
    by_token = P(("dp", "fsdp"), "ctx", None)
    by_row = P(("dp", "ctx", "fsdp"), None)
    in_specs = (by_token, P(("dp", "fsdp"), "ctx"), by_token) + (by_row,) * 21 + (P(),) * 3
    out_specs = (by_token, by_token) + (by_row,) * 21 + (P(),) * 4
    return jax.shard_map(
        partial(body, plan), mesh=mesh, in_specs=in_specs, out_specs=out_specs, check_vma=False
    )
```
